32 devices in a mesh: node: 4 (over y, x), dev: 8 (over z, core).
Axes of the slice: x: 2, y: 2, z: 4, core: 2. Of those that a mesh axis runs over, the one named last changes fastest.
Arguments:
- state: float32 [72, 8, 8192], P(None, None, ('node', 'dev')), may hold values from -6 to 6
- span_owner: int32 [8192, 1], P(('node', 'dev')), may hold values from 0 to 31; in each aligned block of 256 rows (0 to 255, 256 to 511, ...) at most 16 rows name the same one
- regime: int32 [8192], P(('node', 'dev')), may hold values from 0 to 2
- moments: float32 [72, 8, 16384], P(None, None, ('node', 'dev')), may hold values from -6 to 6
- remap_weights: float32 [128, 128, 128], P(('node', 'dev')), may hold values from -0.5 to 0.5
- remap_rows: int32 [128], P(('node', 'dev')), may hold values from 0 to 127
- remap_cols: int32 [128], P(('node', 'dev')), may hold values from 0 to 1
Outputs:
- tendencies: float32 [72, 8, 8192], P(None, None, ('node', 'dev'))
- moments_out: float32 [72, 8, 16384], P(None, None, ('node', 'dev'))
- ocean_flux: float32 [128, 4, 128], P(('node', 'dev'))
The draws below stay inside these ranges and needn't reach their ends.
Inputs may be any that keep to these rules, and one draw needn't show every extreme that they name: `span_owner`: among the 256 columns of one device no owner is named more than 16 times; some device names some owner exactly 16 times.
All inputs are finite; a program needn't handle non-finite values.
Results may differ from the reference program's by a relative error of at most 0.00014.
Values sent between devices are 32-bit elements; how exact they have to be, the bound alone decides.
A program may use at most 64 MiB of HBM per device.

```python
import math
import jax
import jax.numpy as jnp
import numpy as np
from jax import lax

LEV = 72
FLD = 8
MOM = 8
TILE = 128
MICRO_SUB = 2
TURB_ITERS = 3
COL_DEV = 256
PEERS = 32
COLS = 8192
CAP = 16
SLOTS = 16384
ABLK = 2
NBLK_DEV = 4
NBLK = 128
OCN_BLOCKS = 128


def draw_moments(key, part):
    key_base = jax.random.fold_in(key, 11)
    key_offset = jax.random.fold_in(key, 23)
    key_noise = jax.random.fold_in(key, 37)
    base = jnp.clip(jax.random.normal(key_base, (LEV, MOM, SLOTS), jnp.float32), -6.0, 6.0)
    offset = jax.random.uniform(key_offset, (SLOTS,), jnp.float32, -2.5, 2.5)
    noise = 0.7 * jnp.clip(jax.random.normal(key_noise, (LEV, SLOTS), jnp.float32), -2.5, 2.5)
    first = offset[None, :] + noise
    return jnp.concatenate([first[:, None, :], base[:, 1:, :]], axis=1).astype(jnp.float32)


def touch_ends(values, rng, least, largest):
    extent = values.shape
    index_at = [jax.random.randint(jax.random.fold_in(rng, axis), (), 0, extent[axis]) for axis in range(len(extent))]
    values = values.at[tuple(index_at)].set(least)
    longest = extent.index(max(extent))
    index_at[longest] = (index_at[longest] + 1) % extent[longest]
    return values.at[tuple(index_at)].set(largest)


def levels(rng, dims, shards, smallest, top_value):
    level = 1.0
    for axis_at, shards_of in shards:
        draws = jax.random.uniform(jax.random.fold_in(jax.random.fold_in(rng, 6), axis_at), (shards_of,), jnp.float32, smallest / len(shards), top_value / len(shards))
        level = level * jnp.repeat(jnp.exp(draws), dims[axis_at] // shards_of).reshape((-1,) + (1,) * (len(dims) - 1 - axis_at))
    return level


def deal_out(own_key, own, number, rows, number_of, top, most, skew):
    ranking = jax.random.permutation(own_key, number_of)
    crowded, usual = shares(number_of, rows * top, most, skew, True), shares(number_of, rows * top, most, skew, False)
    places = jnp.arange(number_of)

    def named(lengths, rotation):
        used = int((lengths > 0).sum())
        fixed = max(1, used // 4)
        passed = fixed + (places - fixed + rotation * (used - fixed)) % max(1, number_of - fixed)
        return jnp.zeros((number_of,), jnp.int32).at[ranking[jnp.where(places < fixed, places, passed)]].set(jnp.asarray(lengths, jnp.int32))

    lengths = jnp.where(number % 4 == 0, named(crowded, number // 4), named(usual, number - number // 4 - 1))
    mixed = jax.random.permutation(jax.random.fold_in(own, 3), number_of)
    giver, sink = mixed[0:number_of // 2 * 2:2], mixed[1:number_of // 2 * 2:2]
    room = jnp.minimum(lengths[giver] - 1, most - lengths[sink]) // 2
    room = jnp.where((giver == ranking[0]) | (sink == ranking[0]) | (lengths[sink] == 0), 0, jnp.maximum(room, 0))
    passed = jax.random.randint(jax.random.fold_in(own, 4), (number_of // 2,), 0, 1 << 20) % (room + 1)
    lengths = lengths.at[giver].add(-passed).at[sink].add(passed)
    items = jnp.searchsorted(jnp.cumsum(lengths), jnp.arange(rows * top), side="right").astype(jnp.int32)
    listing = items.reshape(top, rows).T
    listing = listing[jax.random.permutation(jax.random.fold_in(own, 1), rows)]
    rotation = jax.random.randint(jax.random.fold_in(own, 2), (rows, 1), 0, top)
    return jnp.take_along_axis(listing, (jnp.arange(top)[None, :] + rotation) % top, axis=1)


def shares(number_of, total, bound, skew, full):
    portions = [(1 << 20) // math.isqrt(standing ** skew) + 1 for standing in range(1, number_of + 1)]
    largest = bound if full else min(bound, max(-(-total // number_of), total * portions[0] // sum(portions)))
    least = 1 if total - largest >= number_of - 1 else 0
    counts, spare = [largest] + [least] * (number_of - 1), total - largest - least * (number_of - 1)
    while spare > 0:
        free = [i for i in range(1, number_of) if counts[i] < largest] or [i for i in range(1, number_of) if counts[i] < bound]
        pool, remaining = sum([portions[i] for i in free]), spare
        for i in free:
            more = min(bound - counts[i], max(1, remaining * portions[i] // pool), spare)
            counts[i] = counts[i] + more
            spare = spare - more
    return np.array(counts)


def gaussian(key, dims, spread, most, split=(), held_as=jnp.bfloat16):
    level = levels(key, dims, split, -0.22, 0.18) if split else 1.0
    drawn = jax.random.normal(key, dims, jnp.float32) * spread * level
    return jnp.minimum(jnp.maximum(drawn, -most), most).astype(held_as)


def setup_inputs(seed: int = 0) -> dict:
    arg_keys = jax.random.split(jax.random.key(seed), 8)
    state = gaussian(arg_keys[0], (LEV, FLD, COLS), 1.0, 6.0, ((2, 32),), jnp.float32)
    span_owner_keys = jax.random.split(jax.random.fold_in(arg_keys[1], 1), COLS // COL_DEV)
    span_owner_turns = jax.random.permutation(jax.random.fold_in(arg_keys[1], 3), COLS // COL_DEV)
    span_owner = jax.vmap(lambda own, number: deal_out(jax.random.fold_in(arg_keys[1], 2), own, number, COL_DEV, PEERS, 1, CAP, 1))(span_owner_keys, span_owner_turns).reshape((COLS, 1))
    regime = touch_ends(jax.random.randint(arg_keys[2], (COLS,), 0, 3), jax.random.fold_in(arg_keys[2], 1), 0, 2).astype(jnp.int32)
    moments = draw_moments(jax.random.fold_in(arg_keys[7], 71), 0)
    remap_weights = gaussian(arg_keys[4], (NBLK, TILE, TILE), TILE ** -0.5, 0.5, ((0, 32),), jnp.float32)
    remap_rows = touch_ends(jax.random.randint(arg_keys[5], (NBLK,), 0, OCN_BLOCKS), jax.random.fold_in(arg_keys[5], 1), 0, OCN_BLOCKS - 1).astype(jnp.int32)
    remap_cols = touch_ends(jax.random.randint(arg_keys[6], (NBLK,), 0, ABLK), jax.random.fold_in(arg_keys[6], 1), 0, ABLK - 1).astype(jnp.int32)
    return {"state": state, "span_owner": span_owner, "regime": regime, "moments": moments, "remap_weights": remap_weights, "remap_rows": remap_rows, "remap_cols": remap_cols}


def level_grad(field):
    padded = jnp.concatenate([field[:1], field, field[-1:]], axis=0)
    return padded[:-2] - padded[2:]

def microphysics(current, column_moments, regime_real):
    temper = current[:, 0]
    vapour = jax.nn.softplus(current[:, 1])
    liquid = jax.nn.softplus(current[:, 2])
    rain_q = jax.nn.softplus(current[:, 3])
    ice_q = jax.nn.softplus(current[:, 4])
    satur = 0.6 * jnp.exp(0.5 * jnp.tanh(0.5 * temper))
    cloudy = 0.5 + jax.nn.sigmoid(column_moments[:, 2] + vapour - satur)
    conden = 0.4 * jnp.tanh(vapour - satur) * cloudy
    autoconv = 0.3 * liquid * liquid / (1.0 + liquid)
    evapor = 0.1 * rain_q * jax.nn.sigmoid(satur - vapour)
    freeze = 0.3 * liquid * jax.nn.sigmoid(-temper)
    melting = 0.2 * ice_q * jax.nn.sigmoid(temper)
    deposit = 0.35 * jnp.tanh(vapour - 0.8 * satur) * cloudy
    aggreg = 0.25 * ice_q * ice_q / (1.0 + ice_q)
    is_warm = (regime_real == 0.0).astype(current.dtype)[None, :]
    is_mixed = (regime_real == 1.0).astype(current.dtype)[None, :]
    is_icy = (regime_real == 2.0).astype(current.dtype)[None, :]
    falling = 0.5 * rain_q
    from_above = jnp.concatenate([jnp.zeros_like(falling[:1]), falling[:-1]], axis=0)
    d_temp = is_warm * (0.8 * (conden - evapor)) + is_mixed * (0.8 * conden + 0.5 * (freeze - melting)) + is_icy * (deposit + 0.5 * freeze)
    d_vapour = is_warm * (evapor - conden) - is_mixed * conden - is_icy * deposit
    d_liquid = is_warm * (conden - autoconv) + is_mixed * (conden - freeze - autoconv) - is_icy * freeze
    d_rain = is_warm * (autoconv - evapor) + is_mixed * (autoconv + melting) + is_icy * aggreg + from_above - falling
    d_ice = is_mixed * (freeze - melting) + is_icy * (deposit + freeze - aggreg)
    return jnp.stack([temper + 0.5 * d_temp, current[:, 1] + 0.5 * d_vapour, current[:, 2] + 0.5 * d_liquid, current[:, 3] + 0.5 * d_rain, current[:, 4] + 0.5 * d_ice, current[:, 5], current[:, 6], current[:, 7]], axis=1)

def diffusivity(mixed_state, column_moments):
    diff_u = mixed_state[:-1, 5] - mixed_state[1:, 5]
    diff_v = mixed_state[:-1, 6] - mixed_state[1:, 6]
    diff_t = mixed_state[:-1, 0] - mixed_state[1:, 0]
    shear_sq = diff_u * diff_u + diff_v * diff_v
    energy = 0.5 + 60.0 * jax.nn.sigmoid(2.0 * (column_moments[:-1, 0] + column_moments[1:, 0]))
    return (0.3 + 1.5 * shear_sq / (1.0 + shear_sq) * jax.nn.sigmoid(-2.0 * diff_t)) * energy

def implicit(kappa_int, right_side):
    zero_row = jnp.zeros_like(kappa_int[:1])
    below_k = jnp.concatenate([zero_row, kappa_int], axis=0)
    above_k = jnp.concatenate([kappa_int, zero_row], axis=0)

    def forward(carry, inputs):
        c_prev, d_prev = carry
        k_low, k_high, rhs_row = inputs
        denominator = 1.0 + k_low + k_high + k_low * c_prev
        c_now = -k_high / denominator
        d_now = (rhs_row + k_low[None, :] * d_prev) / denominator[None, :]
        return ((c_now, d_now), (c_now, d_now))
    start_carry = (jnp.zeros_like(kappa_int[0]), jnp.zeros_like(right_side[0]))
    _, (c_rows, d_rows) = lax.scan(forward, start_carry, (below_k, above_k, right_side))

    def backward(y_next, inputs):
        c_now, d_now = inputs
        y_now = d_now - c_now[None, :] * y_next
        return (y_now, y_now)
    _, solved = lax.scan(backward, jnp.zeros_like(right_side[0]), (c_rows, d_rows), reverse=True)
    return solved

def turbulence(after_micro, column_moments):
    right_side = jnp.concatenate([after_micro[:, 0:2], after_micro[:, 5:8]], axis=1)
    mixed_state = after_micro
    for iteration in range(TURB_ITERS):
        kappa_int = diffusivity(mixed_state, column_moments)
        solved = implicit(kappa_int, right_side)
        mixed_state = jnp.concatenate([solved[:, 0:2], after_micro[:, 2:5], solved[:, 2:5]], axis=1)
    return mixed_state

def update_moments(mixed_state, column_moments):
    grad_u = level_grad(mixed_state[:, 5])
    grad_v = level_grad(mixed_state[:, 6])
    grad_t = level_grad(mixed_state[:, 0])
    grad_q = level_grad(mixed_state[:, 1])
    production = [grad_u * grad_u + grad_v * grad_v, grad_t * grad_t, grad_q * grad_q, grad_t * grad_q, grad_u * grad_t, grad_v * grad_t, grad_u * grad_q, grad_u * grad_v]
    updated = [column_moments[:, index] + 0.5 * (jnp.tanh(production[index]) - (0.3 + 0.1 * index) * column_moments[:, index]) for index in range(8)]
    return jnp.stack(updated, axis=1)

def physics(columns, column_moments, regime_real):
    after_micro = columns
    for substep in range(MICRO_SUB):
        after_micro = microphysics(after_micro, column_moments, regime_real)
    mixed_state = turbulence(after_micro, column_moments)
    return (mixed_state - columns, update_moments(mixed_state, column_moments))

def surface(state, tendencies):
    bottom = state[-1] + tendencies[-1]
    wind_speed = jnp.sqrt(1.0 + bottom[5] * bottom[5] + bottom[6] * bottom[6])
    return jnp.stack([-0.5 * wind_speed * bottom[5], -0.5 * wind_speed * bottom[6], 0.5 * jax.nn.softplus(bottom[3]), -0.3 * wind_speed * bottom[0]], axis=0)

def reference(state, span_owner, regime, moments, remap_weights, remap_rows, remap_cols):
    owners_all = span_owner[:, 0]
    regime_all = regime.astype(jnp.float32)

    def device_block(index, carry):
        tend_all, moments_new = carry
        device = jnp.asarray(index).astype(jnp.int32)
        begin = device * COL_DEV
        columns = lax.dynamic_slice_in_dim(state, begin, COL_DEV, 2)
        owner_ids = lax.dynamic_slice_in_dim(owners_all, begin, COL_DEV, 0).astype(jnp.int32)
        kinds = lax.dynamic_slice_in_dim(regime_all, begin, COL_DEV, 0)
        one_hot = (owner_ids[:, None] == jnp.arange(PEERS, dtype=jnp.int32)[None, :]).astype(jnp.int32)
        rank_in = lax.optimization_barrier(jnp.sum((jnp.cumsum(one_hot, axis=0) - one_hot) * one_hot, axis=1)).astype(jnp.int32)
        global_slot = owner_ids * (CAP * PEERS) + rank_in * PEERS + device
        column_moments = jnp.take(moments, global_slot, axis=2)
        tend_block, new_block = physics(columns, column_moments, kinds)
        tend_all = lax.dynamic_update_slice_in_dim(tend_all, tend_block, begin, 2)
        moments_new = moments_new.at[:, :, global_slot].set(new_block)
        return (tend_all, moments_new)
    tendencies, moments_out = lax.fori_loop(0, PEERS, device_block, (jnp.zeros_like(state), moments))
    fluxes = surface(state, tendencies)
    flux_blocks = fluxes.reshape(4, COLS // TILE, TILE)
    block_ids = jnp.arange(NBLK, dtype=jnp.int32) // NBLK_DEV * ABLK + remap_cols.astype(jnp.int32)
    gathered = flux_blocks[:, block_ids]
    products = jnp.einsum('fbt,bts->bfs', gathered, remap_weights, precision=lax.Precision.HIGHEST)
    ocean_flux = jnp.zeros((OCN_BLOCKS, 4, TILE), dtype=remap_weights.dtype).at[remap_rows].add(products)
    return (tendencies, moments_out, ocean_flux)
```

```python
import functools

import jax
import jax.numpy as jnp
from jax import lax
from jax.experimental import pallas as pl
from jax.experimental.pallas import tpu as pltpu
from jax.sharding import PartitionSpec as P

MICRO_SUB = 2
TURB_ITERS = 3
OBLK_DEV = 4
LANE = 128
SUB = 8
FLUX = 4
GRAD_FIELDS = (5, 6, 0, 1)
F32 = jnp.float32
BF16 = jnp.bfloat16


def plan(peers, cap, levels):
    fetch_rest = 2 * levels - LANE
    back_rest = len(GRAD_FIELDS) * levels - 2 * LANE
    main = max(SUB, cap)
    fetch_rows = max(1, cap * fetch_rest // LANE)
    back_rows = max(1, cap * back_rest // LANE)
    return dict(
        peers=peers,
        cap=cap,
        levels=levels,
        main=main,
        fetch_rest=fetch_rest,
        back_rest=back_rest,
        fetch_rows=fetch_rows,
        back_rows=back_rows,
        fetch_stride=main + SUB,
        back_stride=2 * main + SUB + OBLK_DEV * FLUX,
    )


def sigmoid(x):
    return 0.5 * jnp.tanh(0.5 * x) + 0.5


def softplus(x):
    return jnp.maximum(x, 0.0) + jnp.log(1.0 + jnp.exp(-jnp.abs(x)))


def inverse(x):
    first = pl.reciprocal(x, approx=True)
    return first * (2.0 - x * first)


def split(x):
    high = x.astype(BF16)
    return high, (x - high.astype(F32)).astype(BF16)


def blocks_of(ref, count):
    rows = ref.shape[0] // count
    return [ref.at[pl.ds(block * rows, rows), :] for block in range(count)]


def read_plane(refs, start, rows, stride):
    return jnp.concatenate([ref[pl.ds(start, rows, stride=stride), :] for ref in refs], axis=1)


def write_plane(refs, start, stride, value):
    for block, ref in enumerate(refs):
        ref[pl.ds(start, value.shape[0], stride=stride), :] = value[
            :, block * LANE : (block + 1) * LANE
        ]


def read_tile(refs, cut):
    return jnp.concatenate([ref[cut, :] for ref in refs], axis=1)


def write_tile(refs, cut, value):
    for block, ref in enumerate(refs):
        ref[cut, :] = value[:, block * LANE : (block + 1) * LANE]


def pack_kernel(cfg, *refs):
    levels, peers, cap = cfg["levels"], cfg["peers"], cfg["cap"]
    stride = cfg["fetch_stride"]
    out_ref = refs[-1]
    flat = [ref.reshape(levels * SUB, LANE) for ref in refs[:-1]]
    first = read_plane(flat, 0, levels, SUB)
    third = read_plane(flat, 2, levels, SUB)
    cut = LANE - levels
    main = jnp.concatenate([third, first[:cut]], axis=0).T
    rest = first[cut:]
    for slot in range(cap):
        out_ref[pl.ds(slot, peers, stride=stride), :] = main[slot * peers : (slot + 1) * peers]
    rows = cfg["fetch_rows"]
    groups = cap // rows
    width = rows * peers
    stacked = jnp.concatenate(
        [rest[:, group * width : (group + 1) * width] for group in range(groups)], axis=0
    )
    if stacked.shape[0] < LANE:
        stacked = jnp.concatenate(
            [stacked, jnp.zeros((LANE - stacked.shape[0], width), F32)], axis=0
        )
    if width < LANE:
        stacked = jnp.concatenate([stacked, jnp.zeros((LANE, LANE - width), F32)], axis=1)
    turned = stacked.T
    blank = jnp.zeros((peers, LANE), F32)
    for row in range(cap, cfg["main"]):
        out_ref[pl.ds(row, peers, stride=stride), :] = blank
    for row in range(SUB):
        value = turned[row * peers : (row + 1) * peers] if row < rows else blank
        out_ref[pl.ds(cfg["main"] + row, peers, stride=stride), :] = value


def kappa_tiles(cfg, y_ref, energy_ref, kappa_ref):
    levels = cfg["levels"]
    for tile in range(levels // SUB):
        rows = pl.ds(tile * SUB, SUB)
        here = tile * SUB * SUB

        def drop(field):
            return read_plane(y_ref, here + field, SUB, SUB) - read_plane(
                y_ref, here + SUB + field, SUB, SUB
            )

        diff_u, diff_v, diff_t = drop(5), drop(6), drop(0)
        shear = diff_u * diff_u + diff_v * diff_v
        kappa = (0.3 + 1.5 * shear * inverse(1.0 + shear) * sigmoid(-2.0 * diff_t)) * energy_ref[
            rows, :
        ]
        if tile == levels // SUB - 1:
            level = lax.broadcasted_iota(jnp.int32, kappa.shape, 0)
            kappa = jnp.where(level == SUB - 1, 0.0, kappa)
        kappa_ref[rows, :] = kappa


def solve(cfg, a_ref, kappa_ref, ratio_ref, y_ref):
    levels = cfg["levels"]
    half = levels // 2
    columns = kappa_ref.shape[1]
    zero = jnp.zeros((SUB, columns), F32)

    def tile(level):
        return pl.ds(level * SUB, SUB)

    def kappa_row(level):
        return jnp.broadcast_to(kappa_ref[pl.ds(level, 1), :], (SUB, columns))

    state_of = {0: (zero, zero, zero), 1: (zero, zero, zero)}
    for step in range(half):
        for side in (0, 1):
            level = step if side == 0 else levels - 1 - step
            k_behind, ratio, value = state_of[side]
            k_ahead = kappa_row(level if side == 0 else level - 1)
            scale = inverse((1.0 + k_behind + k_ahead) - k_behind * ratio)
            value = (read_tile(a_ref, tile(level)) + k_behind * value) * scale
            ratio = k_ahead * scale
            write_tile(ratio_ref, tile(level), ratio)
            write_tile(y_ref, tile(level), value)
            state_of[side] = (k_ahead, ratio, value)
    _, ratio_up, value_up = state_of[0]
    _, ratio_low, value_low = state_of[1]
    scale = inverse(1.0 - ratio_up * ratio_low)
    upper = (value_up + ratio_up * value_low) * scale
    lower = (value_low + ratio_low * value_up) * scale
    write_tile(y_ref, tile(half - 1), upper)
    write_tile(y_ref, tile(half), lower)
    for step in range(1, half):
        level = half - 1 - step
        upper = read_tile(y_ref, tile(level)) + read_tile(ratio_ref, tile(level)) * upper
        write_tile(y_ref, tile(level), upper)
        level = half + step
        lower = read_tile(y_ref, tile(level)) + read_tile(ratio_ref, tile(level)) * lower
        write_tile(y_ref, tile(level), lower)


def micro_step(fields, third, above, warm, mixed):
    temper, raw_v, raw_c, raw_r, raw_i = fields
    vapour, liquid, rain_q, ice_q = (softplus(raw) for raw in (raw_v, raw_c, raw_r, raw_i))
    satur = 0.6 * jnp.exp(0.5 * jnp.tanh(0.5 * temper))
    excess = vapour - satur
    cloudy = 0.5 + sigmoid(third + excess)
    conden = 0.4 * jnp.tanh(excess) * cloudy
    autoconv = 0.3 * liquid * liquid * inverse(1.0 + liquid)
    evapor = 0.1 * rain_q * sigmoid(-excess)
    warmth = sigmoid(temper)
    freeze = 0.3 * liquid * (1.0 - warmth)
    melting = 0.2 * ice_q * warmth
    deposit = 0.35 * jnp.tanh(vapour - 0.8 * satur) * cloudy
    aggreg = 0.25 * ice_q * ice_q * inverse(1.0 + ice_q)
    falling = 0.5 * rain_q
    rolled = pltpu.roll(falling, 1, 0)
    level = lax.broadcasted_iota(jnp.int32, falling.shape, 0)
    from_above = jnp.where(level == 0, above, rolled)

    def choose(first, second, last):
        return jnp.where(warm, first, jnp.where(mixed, second, last))

    change = freeze - melting
    d_temp = choose(0.8 * (conden - evapor), 0.8 * conden + 0.5 * change, deposit + 0.5 * freeze)
    d_vapour = choose(evapor - conden, -conden, -deposit)
    d_liquid = choose(conden - autoconv, conden - freeze - autoconv, -freeze)
    d_rain = choose(autoconv - evapor, autoconv + melting, aggreg) + from_above - falling
    d_ice = choose(jnp.zeros_like(change), change, deposit + freeze - aggreg)
    after = tuple(
        value + 0.5 * delta
        for value, delta in zip(fields, (d_temp, d_vapour, d_liquid, d_rain, d_ice))
    )
    return after, rolled


def gather_moments(cfg, fetched, owner_col, rank_col, rank_row):
    levels = cfg["levels"]
    rows, stride = cfg["fetch_rows"], cfg["fetch_stride"]
    columns = owner_col.shape[0]
    place = lax.broadcasted_iota(jnp.int32, (columns, fetched.shape[0]), 1)
    main_at = owner_col * stride + rank_col
    rest_at = owner_col * stride + cfg["main"] + rank_col % rows
    pick = jnp.concatenate(
        [(place == main_at).astype(F32), (place == rest_at).astype(F32)], axis=0
    ).astype(BF16)
    high, low = split(fetched)
    both = jnp.dot(pick, jnp.concatenate([high, low], axis=1), preferred_element_type=F32)
    found = (both[:, :LANE] + both[:, LANE:]).T
    main, rest = found[:, :columns], found[:, columns:]
    size = cfg["fetch_rest"]
    total = jnp.zeros((size, columns), F32)
    for group in range(cfg["cap"] // rows):
        total = total + jnp.where(
            rank_row // rows == group, rest[group * size : (group + 1) * size], 0.0
        )
    third = main[:levels]
    first = jnp.concatenate([main[levels:], total], axis=0)
    return first, third


def physics_kernel(
    cfg,
    blocks,
    *refs,
):
    x_refs, refs = refs[:blocks], refs[blocks:]
    (
    fetched_ref,
    owner_col_ref,
    owner_row_ref,
    regime_ref,
    weights_ref,
    rows_ref,
    cols_ref,
    tend_ref,
    out_ref,
    a_ref,
    y_ref,
    ratio_ref,
    kappa_ref,
    energy_ref,
    third_ref,
    grad_ref,
    ) = refs
    levels, peers, cap = cfg["levels"], cfg["peers"], cfg["cap"]
    columns = blocks * LANE
    x_ref = [ref.reshape(levels * SUB, LANE) for ref in x_refs]
    a_ref, y_ref, ratio_ref = (blocks_of(ref, blocks) for ref in (a_ref, y_ref, ratio_ref))
    t_ref = tend_ref.reshape(levels * SUB, columns)

    owner_col, owner_row = owner_col_ref[...], owner_row_ref[...]
    same = owner_col == owner_row
    down = lax.broadcasted_iota(jnp.int32, (columns, columns), 0)
    across = lax.broadcasted_iota(jnp.int32, (columns, columns), 1)
    rank_row = jnp.sum((same & (down < across)).astype(F32), axis=0, keepdims=True).astype(jnp.int32)
    rank_col = jnp.sum((same & (across < down)).astype(F32), axis=1, keepdims=True).astype(jnp.int32)

    first, third = gather_moments(cfg, fetched_ref[...], owner_col, rank_col, rank_row)
    third_ref[...] = third
    below = jnp.concatenate([first[1:], first[-1:]], axis=0)
    energy_ref[...] = 0.5 + 60.0 * sigmoid(2.0 * (first + below))

    warm = regime_ref[...] == 0
    mixed = regime_ref[...] == 1

    def micro(tile, carry):
        base = tile * (SUB * SUB)
        fields = tuple(read_plane(x_ref, base + field, SUB, SUB) for field in range(5))
        moment = third_ref[pl.ds(pl.multiple_of(tile * SUB, SUB), SUB), :]
        above = []
        for step in range(MICRO_SUB):
            fields, rolled = micro_step(fields, moment, carry[step], warm, mixed)
            above.append(rolled)
        for field in range(5):
            write_plane(a_ref, base + field, SUB, fields[field])
        for field in range(5, SUB):
            write_plane(a_ref, base + field, SUB, read_plane(x_ref, base + field, SUB, SUB))
        return tuple(above)

    nothing = jnp.zeros((SUB, columns), F32)
    lax.fori_loop(0, levels // SUB, micro, (nothing,) * MICRO_SUB)

    pad = pl.ds(levels * SUB, SUB)
    write_tile(a_ref, pad, nothing)
    write_tile(y_ref, pad, nothing)
    kappa_tiles(cfg, a_ref, energy_ref, kappa_ref)
    solve(cfg, a_ref, kappa_ref, ratio_ref, y_ref)

    def again(_, carry):
        kappa_tiles(cfg, y_ref, energy_ref, kappa_ref)
        solve(cfg, a_ref, kappa_ref, ratio_ref, y_ref)
        return carry

    lax.fori_loop(1, TURB_ITERS, again, 0)

    last = pl.ds((levels - 1) * SUB, SUB)
    bottom, bottom_a = read_tile(y_ref, last), read_tile(a_ref, last)
    wind = jnp.sqrt(1.0 + bottom[5:6] * bottom[5:6] + bottom[6:7] * bottom[6:7])
    fluxes = jnp.concatenate(
        [
            -0.5 * wind * bottom[5:6],
            -0.5 * wind * bottom[6:7],
            0.5 * softplus(bottom_a[3:4]),
            -0.3 * wind * bottom[0:1],
        ],
        axis=0,
    )
    flux_high = fluxes.astype(BF16).astype(F32)
    doubled = jnp.concatenate([flux_high, fluxes - flux_high], axis=0)
    products = []
    for block in range(weights_ref.shape[0]):
        chosen = jnp.zeros((SUB, LANE), F32)
        for part in range(columns // LANE):
            chosen = jnp.where(
                cols_ref[block] == part, doubled[:, part * LANE : (part + 1) * LANE], chosen
            )
        high, low = split(weights_ref[block])
        wide = jnp.dot(
            chosen.astype(BF16), jnp.concatenate([high, low], axis=1), preferred_element_type=F32
        )
        once = wide[:, :LANE] + wide[:, LANE:]
        once = once + pltpu.roll(once, FLUX, 0)
        products.append(once)
    row_in = lax.broadcasted_iota(jnp.int32, (SUB, LANE), 0) // FLUX
    per_tile = SUB // FLUX
    ocean_at = 2 * cfg["main"] + SUB
    for peer in range(peers):
        for part in range(OBLK_DEV // per_tile):
            target = row_in + (peer * OBLK_DEV + part * per_tile)
            total = jnp.zeros((SUB, LANE), F32)
            for block, product in enumerate(products):
                total = total + jnp.where(target == rows_ref[block], product, 0.0)
            start = peer * cfg["back_stride"] + ocean_at + part * SUB
            out_ref[pl.ds(start, SUB), :] = total

    live = lax.broadcasted_iota(jnp.int32, (SUB, columns), 0) == SUB - 1
    for index, field in enumerate(GRAD_FIELDS):
        for tile in range(levels // SUB):
            here = tile * SUB * SUB + field
            drop = read_plane(y_ref, here, SUB, SUB) - read_plane(y_ref, here + SUB, SUB, SUB)
            if tile == levels // SUB - 1:
                ends = 1.0 if index == len(GRAD_FIELDS) - 1 else 0.0
                drop = jnp.where(live, ends, drop)
            grad_ref[pl.ds(index * levels + tile * SUB, SUB), :] = drop
    main, rows = cfg["main"], cfg["back_rows"]
    down = lax.broadcasted_iota(jnp.int32, (peers * main, columns), 0)
    put = (down == owner_row * main + rank_row).astype(F32).astype(BF16)
    down = lax.broadcasted_iota(jnp.int32, (peers * SUB, columns), 0)
    put_rest = (down == owner_row * SUB + rank_row % rows).astype(F32).astype(BF16)
    turn = (((1,), (1,)), ((), ()))

    def place(onehot, values):
        high, low = split(values)
        both = lax.dot_general(
            onehot, jnp.concatenate([high, low], axis=0), turn, preferred_element_type=F32
        )
        return both[:, :LANE] + both[:, LANE:]

    size = cfg["back_rest"]
    tail = grad_ref[pl.ds(2 * LANE, size), :]
    groups = cap // rows
    spread = jnp.concatenate(
        [jnp.where(rank_row // rows == group, tail, 0.0) for group in range(groups)], axis=0
    )
    sent = [
        (place(put, grad_ref[pl.ds(0, LANE), :]), 0, main),
        (place(put, grad_ref[pl.ds(LANE, LANE), :]), main, main),
        (place(put_rest, spread), 2 * main, SUB),
    ]
    for value, at, count in sent:
        for peer in range(peers):
            out_ref[pl.ds(peer * cfg["back_stride"] + at, count), :] = value[
                peer * count : (peer + 1) * count
            ]

    field_in = lax.broadcasted_iota(jnp.int32, (SUB, columns), 0)
    kept = (field_in >= 2) & (field_in < 5)
    for level in range(levels):
        cut = pl.ds(level * SUB, SUB)
        ended = jnp.where(kept, read_tile(a_ref, cut), read_tile(y_ref, cut))
        t_ref[cut, :] = ended - read_tile(x_ref, cut)


def update_kernel(cfg, moments_ref, back_ref, out_ref, ocean_ref, diff_ref):
    levels, peers, cap = cfg["levels"], cfg["peers"], cfg["cap"]
    stride, main = cfg["back_stride"], cfg["main"]
    count = len(GRAD_FIELDS) * levels
    block = pl.program_id(0)

    @pl.when(block == 0)
    def _():
        ocean_at = 2 * main + SUB
        total = back_ref[pl.ds(ocean_at, OBLK_DEV * FLUX), :]
        for peer in range(1, peers):
            total = total + back_ref[pl.ds(peer * stride + ocean_at, OBLK_DEV * FLUX), :]
        ocean_ref[...] = total

    width = LANE // peers
    for part in range(2):
        rows = [
            back_ref[pl.ds(part * main + block * width + slot, peers, stride=stride), :]
            for slot in range(width)
        ]
        diff_ref[pl.ds(SUB + part * LANE, LANE), :] = jnp.concatenate(rows, axis=0).T
    rows, size = cfg["back_rows"], cfg["back_rest"]
    turned = jnp.concatenate(
        [back_ref[pl.ds(2 * main + row, peers, stride=stride), :] for row in range(rows)], axis=0
    ).T
    tail = jnp.zeros((size, LANE), F32)
    for group in range(cap // rows):
        tail = jnp.where(block == group, turned[group * size : (group + 1) * size], tail)
    diff_ref[pl.ds(SUB + 2 * LANE, size), :] = tail
    diff_ref[pl.ds(0, SUB), :] = jnp.zeros((SUB, LANE), F32)

    m_ref = [moments_ref.reshape(levels * SUB, LANE)]
    o_ref = [out_ref.reshape(levels * SUB, LANE)]
    live = diff_ref[pl.ds(SUB + count - 1, 1), :] > 0.5
    row_in = lax.broadcasted_iota(jnp.int32, (SUB, LANE), 0)
    for tile in range(levels // SUB):
        grads = []
        for index in range(len(GRAD_FIELDS)):
            at = SUB + index * levels + tile * SUB
            here = diff_ref[pl.ds(at, SUB), :]
            if index == len(GRAD_FIELDS) - 1 and tile == levels // SUB - 1:
                here = jnp.where(row_in == SUB - 1, 0.0, here)
            grads.append(here + diff_ref[pl.ds(at - 1, SUB), :])
        grad_u, grad_v, grad_t, grad_q = grads
        production = [
            grad_u * grad_u + grad_v * grad_v,
            grad_t * grad_t,
            grad_q * grad_q,
            grad_t * grad_q,
            grad_u * grad_t,
            grad_v * grad_t,
            grad_u * grad_q,
            grad_u * grad_v,
        ]
        for index, value in enumerate(production):
            at = tile * SUB * SUB + index
            held = read_plane(m_ref, at, SUB, SUB)
            new = held + 0.5 * (jnp.tanh(value) - (0.3 + 0.1 * index) * held)
            write_plane(o_ref, at, SUB, jnp.where(live, new, held))


VMEM = pl.BlockSpec(memory_space=pltpu.VMEM)
SMEM = pl.BlockSpec(memory_space=pltpu.SMEM)


def pick_block(array, block):
    levels, fields, _ = array.shape
    return pl.BlockSpec((levels, fields, LANE), lambda _: (0, 0, block))


def local(state, span_owner, regime, moments, remap_weights, remap_rows, remap_cols):
    peers = lax.axis_size("node") * lax.axis_size("dev")
    levels, fields, columns = state.shape
    slots = moments.shape[2]
    blocks = columns // LANE
    cfg = plan(peers, slots // peers, levels)
    params = pltpu.CompilerParams(vmem_limit_bytes=48 * 1024 * 1024)

    packed = pl.pallas_call(
        functools.partial(pack_kernel, cfg),
        out_shape=jax.ShapeDtypeStruct((peers * cfg["fetch_stride"], LANE), F32),
        grid=(1,),
        in_specs=[pick_block(moments, block) for block in range(slots // LANE)],
        out_specs=VMEM,
        compiler_params=params,
    )(*[moments] * (slots // LANE))
    fetched = lax.all_to_all(packed, ("node", "dev"), split_axis=0, concat_axis=0, tiled=True)
    tendencies, outgoing = pl.pallas_call(
        functools.partial(physics_kernel, cfg, blocks),
        out_shape=(
            jax.ShapeDtypeStruct(state.shape, F32),
            jax.ShapeDtypeStruct((peers * cfg["back_stride"], LANE), F32),
        ),
        grid=(1,),
        in_specs=[pick_block(state, block) for block in range(blocks)] + [VMEM] * 5 + [SMEM] * 2,
        out_specs=(VMEM, VMEM),
        scratch_shapes=[
            pltpu.VMEM((blocks * (levels + 1) * fields, LANE), F32),
            pltpu.VMEM((blocks * (levels + 1) * fields, LANE), F32),
            pltpu.VMEM((blocks * levels * fields, LANE), F32),
            pltpu.VMEM((levels, columns), F32),
            pltpu.VMEM((levels, columns), F32),
            pltpu.VMEM((levels, columns), F32),
            pltpu.VMEM((len(GRAD_FIELDS) * levels, columns), F32),
        ],
        compiler_params=params,
    )(
        *[state] * blocks,
        fetched,
        span_owner,
        span_owner.reshape(1, columns),
        regime.reshape(1, columns),
        remap_weights,
        remap_rows,
        remap_cols,
    )
    back = lax.all_to_all(outgoing, ("node", "dev"), split_axis=0, concat_axis=0, tiled=True)
    moments_out, ocean = pl.pallas_call(
        functools.partial(update_kernel, cfg),
        out_shape=(
            jax.ShapeDtypeStruct(moments.shape, F32),
            jax.ShapeDtypeStruct((OBLK_DEV * FLUX, LANE), F32),
        ),
        grid=(slots // LANE,),
        in_specs=[pl.BlockSpec((levels, fields, LANE), lambda block: (0, 0, block)), VMEM],
        out_specs=(pl.BlockSpec((levels, fields, LANE), lambda block: (0, 0, block)), VMEM),
        scratch_shapes=[pltpu.VMEM((SUB + len(GRAD_FIELDS) * levels, LANE), F32)],
        compiler_params=params,
    )(moments, back)
    return (tendencies, moments_out, ocean.reshape(OBLK_DEV, FLUX, LANE))


def solution(mesh):
    return jax.shard_map(
        local,
        mesh=mesh,
        in_specs=(
            P(None, None, ("node", "dev")),
            P(("node", "dev"), None),
            P(("node", "dev")),
            P(None, None, ("node", "dev")),
            P(("node", "dev"), None, None),
            P(("node", "dev")),
            P(("node", "dev")),
        ),
        out_specs=(
            P(None, None, ("node", "dev")),
            P(None, None, ("node", "dev")),
            P(("node", "dev"), None, None),
        ),
        check_vma=False,
    )
```

```python
import functools

import jax
import jax.numpy as jnp
from jax import lax
from jax.experimental import pallas as pl
from jax.experimental.pallas import tpu as pltpu
from jax.sharding import PartitionSpec as P

MICRO_SUB = 2
TURB_ITERS = 3
OBLK_DEV = 4
LANE = 128
SUB = 8
FLUX = 4
GRAD_FIELDS = (5, 6, 0, 1)
F32 = jnp.float32
BF16 = jnp.bfloat16


def plan(peers, cap, levels):
    fetch_rest = 2 * levels - LANE
    back_rest = len(GRAD_FIELDS) * levels - 2 * LANE
    main = max(SUB, cap)
    fetch_rows = max(1, cap * fetch_rest // LANE)
    back_rows = max(1, cap * back_rest // LANE)
    return dict(
        peers=peers,
        cap=cap,
        levels=levels,
        main=main,
        fetch_rest=fetch_rest,
        back_rest=back_rest,
        fetch_rows=fetch_rows,
        back_rows=back_rows,
        fetch_stride=main + SUB,
        back_stride=2 * main + SUB,
    )


def sigmoid(x):
    return 0.5 * jnp.tanh(0.5 * x) + 0.5


def softplus(x):
    return jnp.maximum(x, 0.0) + jnp.log(1.0 + jnp.exp(-jnp.abs(x)))


def inverse(x):
    first = pl.reciprocal(x, approx=True)
    return first * (2.0 - x * first)


def split(x):
    high = x.astype(BF16)
    return high, (x - high.astype(F32)).astype(BF16)


def blocks_of(ref, count):
    rows = ref.shape[0] // count
    return [ref.at[pl.ds(block * rows, rows), :] for block in range(count)]


def read_plane(refs, start, rows, stride):
    return jnp.concatenate([ref[pl.ds(start, rows, stride=stride), :] for ref in refs], axis=1)


def write_plane(refs, start, stride, value):
    for block, ref in enumerate(refs):
        ref[pl.ds(start, value.shape[0], stride=stride), :] = value[
            :, block * LANE : (block + 1) * LANE
        ]


def read_tile(refs, cut):
    return jnp.concatenate([ref[cut, :] for ref in refs], axis=1)


def write_tile(refs, cut, value):
    for block, ref in enumerate(refs):
        ref[cut, :] = value[:, block * LANE : (block + 1) * LANE]


def pack(cfg, moment_refs, out_ref):
    levels, peers, cap = cfg["levels"], cfg["peers"], cfg["cap"]
    stride = cfg["fetch_stride"]
    flat = [ref.reshape(levels * SUB, LANE) for ref in moment_refs]
    first = read_plane(flat, 0, levels, SUB)
    third = read_plane(flat, 2, levels, SUB)
    cut = LANE - levels
    main = jnp.concatenate([third, first[:cut]], axis=0).T
    rest = first[cut:]
    for slot in range(cap):
        out_ref[pl.ds(slot, peers, stride=stride), :] = main[slot * peers : (slot + 1) * peers]
    rows = cfg["fetch_rows"]
    groups = cap // rows
    width = rows * peers
    stacked = jnp.concatenate(
        [rest[:, group * width : (group + 1) * width] for group in range(groups)], axis=0
    )
    if stacked.shape[0] < LANE:
        stacked = jnp.concatenate(
            [stacked, jnp.zeros((LANE - stacked.shape[0], width), F32)], axis=0
        )
    if width < LANE:
        stacked = jnp.concatenate([stacked, jnp.zeros((LANE, LANE - width), F32)], axis=1)
    turned = stacked.T
    blank = jnp.zeros((peers, LANE), F32)
    for row in range(cap, cfg["main"]):
        out_ref[pl.ds(row, peers, stride=stride), :] = blank
    for row in range(SUB):
        value = turned[row * peers : (row + 1) * peers] if row < rows else blank
        out_ref[pl.ds(cfg["main"] + row, peers, stride=stride), :] = value


def kappa_tiles(cfg, y_ref, energy_ref, kappa_ref):
    levels = cfg["levels"]
    for tile in range(levels // SUB):
        rows = pl.ds(tile * SUB, SUB)
        here = tile * SUB * SUB

        def drop(field):
            return read_plane(y_ref, here + field, SUB, SUB) - read_plane(
                y_ref, here + SUB + field, SUB, SUB
            )

        diff_u, diff_v, diff_t = drop(5), drop(6), drop(0)
        shear = diff_u * diff_u + diff_v * diff_v
        kappa = (0.3 + 1.5 * shear * inverse(1.0 + shear) * sigmoid(-2.0 * diff_t)) * energy_ref[
            rows, :
        ]
        if tile == levels // SUB - 1:
            level = lax.broadcasted_iota(jnp.int32, kappa.shape, 0)
            kappa = jnp.where(level == SUB - 1, 0.0, kappa)
        kappa_ref[rows, :] = kappa


def solve(cfg, a_ref, kappa_ref, ratio_ref, y_ref):
    levels = cfg["levels"]
    half = levels // 2
    columns = kappa_ref.shape[1]
    zero = jnp.zeros((SUB, columns), F32)

    def tile(level):
        return pl.ds(level * SUB, SUB)

    def kappa_row(level):
        return jnp.broadcast_to(kappa_ref[pl.ds(level, 1), :], (SUB, columns))

    state_of = {0: (zero, zero, zero), 1: (zero, zero, zero)}
    for step in range(half):
        for side in (0, 1):
            level = step if side == 0 else levels - 1 - step
            k_behind, ratio, value = state_of[side]
            k_ahead = kappa_row(level if side == 0 else level - 1)
            scale = inverse((1.0 + k_behind + k_ahead) - k_behind * ratio)
            value = (read_tile(a_ref, tile(level)) + k_behind * value) * scale
            ratio = k_ahead * scale
            write_tile(ratio_ref, tile(level), ratio)
            write_tile(y_ref, tile(level), value)
            state_of[side] = (k_ahead, ratio, value)
    _, ratio_up, value_up = state_of[0]
    _, ratio_low, value_low = state_of[1]
    scale = inverse(1.0 - ratio_up * ratio_low)
    upper = (value_up + ratio_up * value_low) * scale
    lower = (value_low + ratio_low * value_up) * scale
    write_tile(y_ref, tile(half - 1), upper)
    write_tile(y_ref, tile(half), lower)
    for step in range(1, half):
        level = half - 1 - step
        upper = read_tile(y_ref, tile(level)) + read_tile(ratio_ref, tile(level)) * upper
        write_tile(y_ref, tile(level), upper)
        level = half + step
        lower = read_tile(y_ref, tile(level)) + read_tile(ratio_ref, tile(level)) * lower
        write_tile(y_ref, tile(level), lower)


def micro_step(fields, third, above, warm, mixed):
    temper, raw_v, raw_c, raw_r, raw_i = fields
    vapour, liquid, rain_q, ice_q = (softplus(raw) for raw in (raw_v, raw_c, raw_r, raw_i))
    satur = 0.6 * jnp.exp(0.5 * jnp.tanh(0.5 * temper))
    excess = vapour - satur
    cloudy = 0.5 + sigmoid(third + excess)
    conden = 0.4 * jnp.tanh(excess) * cloudy
    autoconv = 0.3 * liquid * liquid * inverse(1.0 + liquid)
    evapor = 0.1 * rain_q * sigmoid(-excess)
    warmth = sigmoid(temper)
    freeze = 0.3 * liquid * (1.0 - warmth)
    melting = 0.2 * ice_q * warmth
    deposit = 0.35 * jnp.tanh(vapour - 0.8 * satur) * cloudy
    aggreg = 0.25 * ice_q * ice_q * inverse(1.0 + ice_q)
    falling = 0.5 * rain_q
    rolled = pltpu.roll(falling, 1, 0)
    level = lax.broadcasted_iota(jnp.int32, falling.shape, 0)
    from_above = jnp.where(level == 0, above, rolled)

    def choose(first, second, last):
        return jnp.where(warm, first, jnp.where(mixed, second, last))

    change = freeze - melting
    d_temp = choose(0.8 * (conden - evapor), 0.8 * conden + 0.5 * change, deposit + 0.5 * freeze)
    d_vapour = choose(evapor - conden, -conden, -deposit)
    d_liquid = choose(conden - autoconv, conden - freeze - autoconv, -freeze)
    d_rain = choose(autoconv - evapor, autoconv + melting, aggreg) + from_above - falling
    d_ice = choose(jnp.zeros_like(change), change, deposit + freeze - aggreg)
    after = tuple(
        value + 0.5 * delta
        for value, delta in zip(fields, (d_temp, d_vapour, d_liquid, d_rain, d_ice))
    )
    return after, rolled


def one_hot_fetch(cfg, owner_col, rank_col):
    rows, stride = cfg["fetch_rows"], cfg["fetch_stride"]
    columns = owner_col.shape[0]
    place = lax.broadcasted_iota(jnp.int32, (columns, cfg["peers"] * stride), 1)
    main_at = owner_col * stride + rank_col
    rest_at = owner_col * stride + cfg["main"] + rank_col % rows
    return jnp.concatenate(
        [(place == main_at).astype(F32), (place == rest_at).astype(F32)], axis=0
    ).astype(BF16)


def gather_moments(cfg, fetched, pick, rank_row):
    levels, rows = cfg["levels"], cfg["fetch_rows"]
    columns = rank_row.shape[1]
    row_in = lax.broadcasted_iota(jnp.int32, fetched.shape, 0) % cfg["fetch_stride"]
    fetched = jnp.where(row_in < cfg["main"] + rows, fetched, 0.0)
    high, low = split(fetched)
    both = jnp.dot(pick, jnp.concatenate([high, low], axis=1), preferred_element_type=F32)
    found = (both[:, :LANE] + both[:, LANE:]).T
    main, rest = found[:, :columns], found[:, columns:]
    size = cfg["fetch_rest"]
    total = jnp.zeros((size, columns), F32)
    for group in range(cfg["cap"] // rows):
        total = total + jnp.where(
            rank_row // rows == group, rest[group * size : (group + 1) * size], 0.0
        )
    third = main[:levels]
    first = jnp.concatenate([main[levels:], total], axis=0)
    return first, third


class Links:
    def __init__(self):
        self.nodes, self.devs = lax.axis_size("node"), lax.axis_size("dev")
        self.node, self.dev = lax.axis_index("node"), lax.axis_index("dev")
        self.me = self.node * self.devs + self.dev

    def coordinates(self, peer):
        return (peer // self.devs, peer % self.devs)


def remote(source, target, sends, receives, step, where):
    return pltpu.make_async_remote_copy(
        src_ref=source,
        dst_ref=target,
        send_sem=sends.at[step],
        recv_sem=receives.at[step],
        device_id=where,
        device_id_type=pl.DeviceIdType.MESH,
    )


def each(start, stop, body):
    def step(index, carry):
        body(index)
        return carry

    lax.fori_loop(start, stop, step, 0)


def step_kernel(cfg, blocks, slot_blocks, *refs):
    x_refs, refs = refs[:blocks], refs[blocks:]
    moment_refs, refs = refs[:slot_blocks], refs[slot_blocks:]
    (
        owner_col_ref,
        owner_row_ref,
        regime_ref,
        weights_ref,
        rows_ref,
        cols_ref,
        tend_ref,
        back_ref,
        ocean_ref,
        packed_ref,
        fetched_ref,
        out_ref,
        plane_ref,
        plane_in_ref,
        column_ref,
        a_ref,
        y_ref,
        ratio_ref,
        kappa_ref,
        energy_ref,
        third_ref,
        grad_ref,
        fetch_send,
        fetch_recv,
        back_send,
        back_recv,
        plane_send,
        plane_recv,
        column_send,
        column_recv,
        own_sem,
        own_ocean_sem,
    ) = refs
    links = Links()
    me = links.me
    barrier = pltpu.get_barrier_semaphore()
    all_peers = cfg["peers"]

    def greet(step):
        pl.semaphore_signal(
            barrier,
            inc=1,
            device_id=links.coordinates((me + step) % all_peers),
            device_id_type=pl.DeviceIdType.MESH,
        )

    each(1, all_peers, greet)
    pack(cfg, moment_refs, packed_ref)
    pl.semaphore_wait(barrier, all_peers - 1)

    def fetch_copy(step):
        peer = (me + step) % all_peers
        count = cfg["main"] + cfg["fetch_rows"]
        return remote(
            packed_ref.at[pl.ds(peer * cfg["fetch_stride"], count), :],
            fetched_ref.at[pl.ds(me * cfg["fetch_stride"], count), :],
            fetch_send,
            fetch_recv,
            step,
            links.coordinates(peer),
        )

    each(1, all_peers, lambda step: fetch_copy(step).start())
    own = pl.ds(pl.multiple_of(me * cfg["fetch_stride"], SUB), cfg["fetch_stride"])
    fetched_ref[own, :] = packed_ref[own, :]

    levels, peers, cap = cfg["levels"], cfg["peers"], cfg["cap"]
    columns = blocks * LANE
    x_ref = [ref.reshape(levels * SUB, LANE) for ref in x_refs]
    a_ref, y_ref, ratio_ref = (blocks_of(ref, blocks) for ref in (a_ref, y_ref, ratio_ref))
    t_ref = tend_ref.reshape(levels * SUB, columns)

    owner_col, owner_row = owner_col_ref[...], owner_row_ref[...]
    same = owner_col == owner_row
    down = lax.broadcasted_iota(jnp.int32, (columns, columns), 0)
    across = lax.broadcasted_iota(jnp.int32, (columns, columns), 1)
    rank_row = jnp.sum((same & (down < across)).astype(F32), axis=0, keepdims=True).astype(jnp.int32)
    rank_col = jnp.sum((same & (across < down)).astype(F32), axis=1, keepdims=True).astype(jnp.int32)

    pick = one_hot_fetch(cfg, owner_col, rank_col)
    each(1, all_peers, lambda step: fetch_copy(step).wait_recv())
    first, third = gather_moments(cfg, fetched_ref[...], pick, rank_row)
    third_ref[...] = third
    below = jnp.concatenate([first[1:], first[-1:]], axis=0)
    energy_ref[...] = 0.5 + 60.0 * sigmoid(2.0 * (first + below))

    warm = regime_ref[...] == 0
    mixed = regime_ref[...] == 1

    def micro(tile, carry):
        base = tile * (SUB * SUB)
        fields = tuple(read_plane(x_ref, base + field, SUB, SUB) for field in range(5))
        moment = third_ref[pl.ds(pl.multiple_of(tile * SUB, SUB), SUB), :]
        above = []
        for step in range(MICRO_SUB):
            fields, rolled = micro_step(fields, moment, carry[step], warm, mixed)
            above.append(rolled)
        fields = fields + tuple(read_plane(x_ref, base + field, SUB, SUB) for field in (5, 6, 7))
        for field in range(SUB):
            write_plane(a_ref, base + field, SUB, fields[field])
            write_plane(y_ref, base + field, SUB, fields[field])
        return tuple(above)

    nothing = jnp.zeros((SUB, columns), F32)
    lax.fori_loop(0, levels // SUB, micro, (nothing,) * MICRO_SUB)

    pad = pl.ds(levels * SUB, SUB)
    write_tile(y_ref, pad, nothing)

    def again(_, carry):
        kappa_tiles(cfg, y_ref, energy_ref, kappa_ref)
        solve(cfg, a_ref, kappa_ref, ratio_ref, y_ref)
        return carry

    lax.fori_loop(0, TURB_ITERS, again, 0)

    last = pl.ds((levels - 1) * SUB, SUB)
    bottom, bottom_a = read_tile(y_ref, last), read_tile(a_ref, last)
    wind = jnp.sqrt(1.0 + bottom[5:6] * bottom[5:6] + bottom[6:7] * bottom[6:7])
    fluxes = jnp.concatenate(
        [
            -0.5 * wind * bottom[5:6],
            -0.5 * wind * bottom[6:7],
            0.5 * softplus(bottom_a[3:4]),
            -0.3 * wind * bottom[0:1],
        ],
        axis=0,
    )
    flux_high = fluxes.astype(BF16).astype(F32)
    doubled = jnp.concatenate([flux_high, fluxes - flux_high], axis=0)
    products = []
    for block in range(weights_ref.shape[0]):
        chosen = jnp.zeros((SUB, LANE), F32)
        for part in range(columns // LANE):
            chosen = jnp.where(
                cols_ref[block] == part, doubled[:, part * LANE : (part + 1) * LANE], chosen
            )
        high, low = split(weights_ref[block])
        wide = jnp.dot(
            chosen.astype(BF16), jnp.concatenate([high, low], axis=1), preferred_element_type=F32
        )
        once = wide[:, :LANE] + wide[:, LANE:]
        once = once + pltpu.roll(once, FLUX, 0)
        products.append(once)
    row_in = lax.broadcasted_iota(jnp.int32, (SUB, LANE), 0) // FLUX
    per_tile = SUB // FLUX
    share = OBLK_DEV * FLUX
    floors = links.devs // 2
    floor, side = links.dev // 2, links.dev % 2
    group = links.nodes * 2
    here = links.node * 2 + side
    span = floors * share
    for member in range(group):
        for level in range(floors):
            owner = member // 2 * links.devs + level * 2 + member % 2
            for part in range(OBLK_DEV // per_tile):
                target = row_in + (owner * OBLK_DEV + part * per_tile)
                total = jnp.zeros((SUB, LANE), F32)
                for block, product in enumerate(products):
                    total = total + jnp.where(target == rows_ref[block], product, 0.0)
                plane_ref[pl.ds(member * span + level * share + part * SUB, SUB), :] = total

    def plane_copy(step):
        member = (here + step) % group
        return remote(
            plane_ref.at[pl.ds(member * span, span), :],
            plane_in_ref.at[pl.ds(here * span, span), :],
            plane_send,
            plane_recv,
            step,
            (member // 2, floor * 2 + member % 2),
        )

    each(1, group, lambda step: plane_copy(step).start())
    mine = pl.ds(pl.multiple_of(here * span, SUB), span)
    plane_in_ref[mine, :] = plane_ref[mine, :]

    live = lax.broadcasted_iota(jnp.int32, (SUB, columns), 0) == SUB - 1
    for index, field in enumerate(GRAD_FIELDS):
        for tile in range(levels // SUB):
            at = tile * SUB * SUB + field
            drop = read_plane(y_ref, at, SUB, SUB) - read_plane(y_ref, at + SUB, SUB, SUB)
            if tile == levels // SUB - 1:
                ends = 1.0 if index == len(GRAD_FIELDS) - 1 else 0.0
                drop = jnp.where(live, ends, drop)
            grad_ref[pl.ds(index * levels + tile * SUB, SUB), :] = drop
    main, rows = cfg["main"], cfg["back_rows"]
    down = lax.broadcasted_iota(jnp.int32, (peers * main, columns), 0)
    put = (down == owner_row * main + rank_row).astype(F32).astype(BF16)
    down = lax.broadcasted_iota(jnp.int32, (peers * SUB, columns), 0)
    put_rest = (down == owner_row * SUB + rank_row % rows).astype(F32).astype(BF16)
    turn = (((1,), (1,)), ((), ()))

    def place(onehot, values):
        high, low = split(values)
        both = lax.dot_general(
            onehot, jnp.concatenate([high, low], axis=0), turn, preferred_element_type=F32
        )
        return both[:, :LANE] + both[:, LANE:]

    size = cfg["back_rest"]
    tail = grad_ref[pl.ds(2 * LANE, size), :]
    groups = cap // rows
    spread = jnp.concatenate(
        [jnp.where(rank_row // rows == group, tail, 0.0) for group in range(groups)], axis=0
    )
    sent = [
        (place(put, grad_ref[pl.ds(0, LANE), :]), 0, main),
        (place(put, grad_ref[pl.ds(LANE, LANE), :]), main, main),
        (place(put_rest, spread), 2 * main, SUB),
    ]
    for value, at, count in sent:
        for peer in range(peers):
            out_ref[pl.ds(peer * cfg["back_stride"] + at, count), :] = value[
                peer * count : (peer + 1) * count
            ]

    def back_copy(step):
        peer = (me + step) % all_peers
        count = 2 * main + rows
        return remote(
            out_ref.at[pl.ds(peer * cfg["back_stride"], count), :],
            back_ref.at[pl.ds(me * cfg["back_stride"], count), :],
            back_send,
            back_recv,
            step,
            links.coordinates(peer),
        )

    each(1, all_peers, lambda step: back_copy(step).start())
    own = pl.ds(pl.multiple_of(me * cfg["back_stride"], SUB), cfg["back_stride"])
    own_copy = pltpu.make_async_copy(out_ref.at[own, :], back_ref.at[own, :], own_sem)
    own_copy.start()

    each(1, group, lambda step: plane_copy(step).wait_recv())
    total = plane_in_ref[pl.ds(0, span), :]
    for member in range(1, group):
        total = total + plane_in_ref[pl.ds(member * span, span), :]
    column_ref[...] = total

    def column_copy(step):
        level = (floor + step) % floors
        return remote(
            column_ref.at[pl.ds(level * share, share), :],
            ocean_ref.at[pl.ds(floor * share, share), :],
            column_send,
            column_recv,
            step,
            (links.node, level * 2 + side),
        )

    each(1, floors, lambda step: column_copy(step).start())
    mine = pl.ds(pl.multiple_of(floor * share, SUB), share)
    own_ocean = pltpu.make_async_copy(column_ref.at[mine, :], ocean_ref.at[mine, :], own_ocean_sem)
    own_ocean.start()

    field_in = lax.broadcasted_iota(jnp.int32, (SUB, columns), 0)
    kept = (field_in >= 2) & (field_in < 5)
    for level in range(levels):
        cut = pl.ds(level * SUB, SUB)
        ended = jnp.where(kept, read_tile(a_ref, cut), read_tile(y_ref, cut))
        t_ref[cut, :] = ended - read_tile(x_ref, cut)

    own_copy.wait()
    own_ocean.wait()
    each(1, all_peers, lambda step: fetch_copy(step).wait_send())
    each(1, group, lambda step: plane_copy(step).wait_send())
    each(1, floors, lambda step: column_copy(step).wait())
    each(1, all_peers, lambda step: back_copy(step).wait())


def update_kernel(cfg, moments_ref, back_ref, parts_ref, out_ref, ocean_ref, diff_ref):
    levels, peers, cap = cfg["levels"], cfg["peers"], cfg["cap"]
    stride, main = cfg["back_stride"], cfg["main"]
    count = len(GRAD_FIELDS) * levels
    block = pl.program_id(0)

    @pl.when(block == 0)
    def _():
        share = OBLK_DEV * FLUX
        total = parts_ref[pl.ds(0, share), :]
        for floor in range(1, parts_ref.shape[0] // share):
            total = total + parts_ref[pl.ds(floor * share, share), :]
        ocean_ref[...] = total

    width = LANE // peers
    for part in range(2):
        rows = [
            back_ref[pl.ds(part * main + block * width + slot, peers, stride=stride), :]
            for slot in range(width)
        ]
        diff_ref[pl.ds(SUB + part * LANE, LANE), :] = jnp.concatenate(rows, axis=0).T
    rows, size = cfg["back_rows"], cfg["back_rest"]
    turned = jnp.concatenate(
        [back_ref[pl.ds(2 * main + row, peers, stride=stride), :] for row in range(rows)], axis=0
    ).T
    tail = jnp.zeros((size, LANE), F32)
    for group in range(cap // rows):
        tail = jnp.where(block == group, turned[group * size : (group + 1) * size], tail)
    diff_ref[pl.ds(SUB + 2 * LANE, size), :] = tail
    diff_ref[pl.ds(0, SUB), :] = jnp.zeros((SUB, LANE), F32)

    m_ref = [moments_ref.reshape(levels * SUB, LANE)]
    o_ref = [out_ref.reshape(levels * SUB, LANE)]
    live = diff_ref[pl.ds(SUB + count - 1, 1), :] > 0.5
    row_in = lax.broadcasted_iota(jnp.int32, (SUB, LANE), 0)
    for tile in range(levels // SUB):
        grads = []
        for index in range(len(GRAD_FIELDS)):
            at = SUB + index * levels + tile * SUB
            here = diff_ref[pl.ds(at, SUB), :]
            if index == len(GRAD_FIELDS) - 1 and tile == levels // SUB - 1:
                here = jnp.where(row_in == SUB - 1, 0.0, here)
            grads.append(here + diff_ref[pl.ds(at - 1, SUB), :])
        grad_u, grad_v, grad_t, grad_q = grads
        production = [
            grad_u * grad_u + grad_v * grad_v,
            grad_t * grad_t,
            grad_q * grad_q,
            grad_t * grad_q,
            grad_u * grad_t,
            grad_v * grad_t,
            grad_u * grad_q,
            grad_u * grad_v,
        ]
        for index, value in enumerate(production):
            at = tile * SUB * SUB + index
            held = read_plane(m_ref, at, SUB, SUB)
            new = held + 0.5 * (jnp.tanh(value) - (0.3 + 0.1 * index) * held)
            write_plane(o_ref, at, SUB, jnp.where(live, new, held))


VMEM = pl.BlockSpec(memory_space=pltpu.VMEM)
SMEM = pl.BlockSpec(memory_space=pltpu.SMEM)


def pick_block(array, block):
    levels, fields, _ = array.shape
    return pl.BlockSpec((levels, fields, LANE), lambda _: (0, 0, block))


def local(state, span_owner, regime, moments, remap_weights, remap_rows, remap_cols):
    peers = lax.axis_size("node") * lax.axis_size("dev")
    levels, fields, columns = state.shape
    slots = moments.shape[2]
    blocks = columns // LANE
    cfg = plan(peers, slots // peers, levels)
    params = pltpu.CompilerParams(vmem_limit_bytes=48 * 1024 * 1024)

    floors = lax.axis_size("dev") // 2
    group = 2 * lax.axis_size("node")
    share = OBLK_DEV * FLUX
    whole = pl.BlockSpec(memory_space=pl.ANY)

    def rows_of(count):
        return pltpu.VMEM((count, LANE), F32)

    def copies_of(count):
        return [pltpu.SemaphoreType.DMA((count,))] * 2

    tendencies, back, parts = pl.pallas_call(
        functools.partial(step_kernel, cfg, blocks, slots // LANE),
        out_shape=(
            jax.ShapeDtypeStruct(state.shape, F32),
            jax.ShapeDtypeStruct((peers * cfg["back_stride"], LANE), F32),
            jax.ShapeDtypeStruct((floors * share, LANE), F32),
        ),
        grid=(1,),
        in_specs=[pick_block(state, block) for block in range(blocks)]
        + [pick_block(moments, block) for block in range(slots // LANE)]
        + [VMEM] * 4
        + [SMEM] * 2,
        out_specs=(VMEM, whole, whole),
        scratch_shapes=[
            rows_of(peers * cfg["fetch_stride"]),
            rows_of(peers * cfg["fetch_stride"]),
            rows_of(peers * cfg["back_stride"]),
            rows_of(group * floors * share),
            rows_of(group * floors * share),
            rows_of(floors * share),
            rows_of(blocks * (levels + 1) * fields),
            rows_of(blocks * (levels + 1) * fields),
            rows_of(blocks * levels * fields),
            pltpu.VMEM((levels, columns), F32),
            pltpu.VMEM((levels, columns), F32),
            pltpu.VMEM((levels, columns), F32),
            pltpu.VMEM((len(GRAD_FIELDS) * levels, columns), F32),
        ]
        + copies_of(peers)
        + copies_of(peers)
        + copies_of(group)
        + copies_of(floors)
        + [pltpu.SemaphoreType.DMA, pltpu.SemaphoreType.DMA],
        compiler_params=pltpu.CompilerParams(
            vmem_limit_bytes=48 * 1024 * 1024, collective_id=0, has_side_effects=True
        ),
    )(
        *[state] * blocks,
        *[moments] * (slots // LANE),
        span_owner,
        span_owner.reshape(1, columns),
        regime.reshape(1, columns),
        remap_weights,
        remap_rows,
        remap_cols,
    )
    moments_out, ocean = pl.pallas_call(
        functools.partial(update_kernel, cfg),
        out_shape=(
            jax.ShapeDtypeStruct(moments.shape, F32),
            jax.ShapeDtypeStruct((OBLK_DEV * FLUX, LANE), F32),
        ),
        grid=(slots // LANE,),
        in_specs=[pl.BlockSpec((levels, fields, LANE), lambda block: (0, 0, block)), VMEM, VMEM],
        out_specs=(pl.BlockSpec((levels, fields, LANE), lambda block: (0, 0, block)), VMEM),
        scratch_shapes=[pltpu.VMEM((SUB + len(GRAD_FIELDS) * levels, LANE), F32)],
        compiler_params=params,
    )(moments, back, parts)
    return (tendencies, moments_out, ocean.reshape(OBLK_DEV, FLUX, LANE))


def solution(mesh):
    return jax.shard_map(
        local,
        mesh=mesh,
        in_specs=(
            P(None, None, ("node", "dev")),
            P(("node", "dev"), None),
            P(("node", "dev")),
            P(None, None, ("node", "dev")),
            P(("node", "dev"), None, None),
            P(("node", "dev")),
            P(("node", "dev")),
        ),
        out_specs=(
            P(None, None, ("node", "dev")),
            P(None, None, ("node", "dev")),
            P(("node", "dev"), None, None),
        ),
        check_vma=False,
    )
```

```python
import functools

import jax
import jax.numpy as jnp
from jax import lax
from jax.experimental import pallas as pl
from jax.experimental.pallas import tpu as pltpu
from jax.sharding import PartitionSpec as P

MICRO_SUB = 2
TURB_ITERS = 3
OBLK_DEV = 4
LANE = 128
SUB = 8
FLUX = 4
VMEM_BYTES = 60 * 1024 * 1024
GRAD_FIELDS = (5, 6, 0, 1)
F32 = jnp.float32
BF16 = jnp.bfloat16


def plan(peers, cap, levels):
    fetch_rest = 2 * levels - LANE
    back_rest = len(GRAD_FIELDS) * levels - 2 * LANE
    main = max(SUB, cap)
    fetch_rows = max(1, cap * fetch_rest // LANE)
    back_rows = max(1, cap * back_rest // LANE)
    return dict(
        peers=peers,
        cap=cap,
        levels=levels,
        main=main,
        fetch_rest=fetch_rest,
        back_rest=back_rest,
        fetch_rows=fetch_rows,
        back_rows=back_rows,
        fetch_stride=main + SUB,
        back_stride=2 * main + SUB,
    )


def sigmoid(x):
    return 0.5 * jnp.tanh(0.5 * x) + 0.5


def softplus(x):
    return jnp.maximum(x, 0.0) + jnp.log(1.0 + jnp.exp(-jnp.abs(x)))


def inverse(x):
    first = pl.reciprocal(x, approx=True)
    return first * (2.0 - x * first)


def split(x):
    high = x.astype(BF16)
    return high, (x - high.astype(F32)).astype(BF16)


def blocks_of(ref, count):
    rows = ref.shape[0] // count
    return [ref.at[pl.ds(block * rows, rows), :] for block in range(count)]


def read_plane(refs, start, rows, stride):
    return jnp.concatenate([ref[pl.ds(start, rows, stride=stride), :] for ref in refs], axis=1)


def write_plane(refs, start, stride, value):
    for block, ref in enumerate(refs):
        ref[pl.ds(start, value.shape[0], stride=stride), :] = value[
            :, block * LANE : (block + 1) * LANE
        ]


def read_tile(refs, cut):
    return jnp.concatenate([ref[cut, :] for ref in refs], axis=1)


def write_tile(refs, cut, value):
    for block, ref in enumerate(refs):
        ref[cut, :] = value[:, block * LANE : (block + 1) * LANE]


def pack(cfg, flat, out_ref):
    levels, peers, cap = cfg["levels"], cfg["peers"], cfg["cap"]
    stride = cfg["fetch_stride"]
    first = read_plane(flat, 0, levels, SUB)
    third = read_plane(flat, 2, levels, SUB)
    cut = LANE - levels
    main = jnp.concatenate([third, first[:cut]], axis=0).T
    rest = first[cut:]
    for slot in range(cap):
        out_ref[pl.ds(slot, peers, stride=stride), :] = main[slot * peers : (slot + 1) * peers]
    rows = cfg["fetch_rows"]
    groups = cap // rows
    width = rows * peers
    stacked = jnp.concatenate(
        [rest[:, group * width : (group + 1) * width] for group in range(groups)], axis=0
    )
    if stacked.shape[0] < LANE:
        stacked = jnp.concatenate(
            [stacked, jnp.zeros((LANE - stacked.shape[0], width), F32)], axis=0
        )
    if width < LANE:
        stacked = jnp.concatenate([stacked, jnp.zeros((LANE, LANE - width), F32)], axis=1)
    turned = stacked.T
    blank = jnp.zeros((peers, LANE), F32)
    for row in range(cap, cfg["main"]):
        out_ref[pl.ds(row, peers, stride=stride), :] = blank
    for row in range(SUB):
        value = turned[row * peers : (row + 1) * peers] if row < rows else blank
        out_ref[pl.ds(cfg["main"] + row, peers, stride=stride), :] = value


def kappa_tiles(cfg, y_ref, energy_ref, kappa_ref):
    levels = cfg["levels"]
    for tile in range(levels // SUB):
        rows = pl.ds(tile * SUB, SUB)
        here = tile * SUB * SUB

        def drop(field):
            return read_plane(y_ref, here + field, SUB, SUB) - read_plane(
                y_ref, here + SUB + field, SUB, SUB
            )

        diff_u, diff_v, diff_t = drop(5), drop(6), drop(0)
        shear = diff_u * diff_u + diff_v * diff_v
        kappa = (0.3 + 1.5 * shear * inverse(1.0 + shear) * sigmoid(-2.0 * diff_t)) * energy_ref[
            rows, :
        ]
        if tile == levels // SUB - 1:
            level = lax.broadcasted_iota(jnp.int32, kappa.shape, 0)
            kappa = jnp.where(level == SUB - 1, 0.0, kappa)
        kappa_ref[rows, :] = kappa


def solve(cfg, a_ref, kappa_ref, ratio_ref, y_ref):
    levels = cfg["levels"]
    half = levels // 2
    columns = kappa_ref.shape[1]
    zero = jnp.zeros((SUB, columns), F32)

    def tile(level):
        return pl.ds(level * SUB, SUB)

    def kappa_row(level):
        return jnp.broadcast_to(kappa_ref[pl.ds(level, 1), :], (SUB, columns))

    state_of = {0: (zero, zero, zero), 1: (zero, zero, zero)}
    for step in range(half):
        for side in (0, 1):
            level = step if side == 0 else levels - 1 - step
            k_behind, ratio, value = state_of[side]
            k_ahead = kappa_row(level if side == 0 else level - 1)
            scale = inverse((1.0 + k_behind + k_ahead) - k_behind * ratio)
            value = (read_tile(a_ref, tile(level)) + k_behind * value) * scale
            ratio = k_ahead * scale
            write_tile(ratio_ref, tile(level), ratio)
            write_tile(y_ref, tile(level), value)
            state_of[side] = (k_ahead, ratio, value)
    _, ratio_up, value_up = state_of[0]
    _, ratio_low, value_low = state_of[1]
    scale = inverse(1.0 - ratio_up * ratio_low)
    upper = (value_up + ratio_up * value_low) * scale
    lower = (value_low + ratio_low * value_up) * scale
    write_tile(y_ref, tile(half - 1), upper)
    write_tile(y_ref, tile(half), lower)
    for step in range(1, half):
        level = half - 1 - step
        upper = read_tile(y_ref, tile(level)) + read_tile(ratio_ref, tile(level)) * upper
        write_tile(y_ref, tile(level), upper)
        level = half + step
        lower = read_tile(y_ref, tile(level)) + read_tile(ratio_ref, tile(level)) * lower
        write_tile(y_ref, tile(level), lower)


def micro_rates(fields, above, warm, mixed):
    temper, raw_v, raw_c, raw_r, raw_i = fields
    vapour, liquid, rain_q, ice_q = (softplus(raw) for raw in (raw_v, raw_c, raw_r, raw_i))
    satur = 0.6 * jnp.exp(0.5 * jnp.tanh(0.5 * temper))
    excess = vapour - satur
    autoconv = 0.3 * liquid * liquid * inverse(1.0 + liquid)
    evapor = 0.1 * rain_q * sigmoid(-excess)
    warmth = sigmoid(temper)
    freeze = 0.3 * liquid * (1.0 - warmth)
    melting = 0.2 * ice_q * warmth
    aggreg = 0.25 * ice_q * ice_q * inverse(1.0 + ice_q)
    falling = 0.5 * rain_q
    rolled = pltpu.roll(falling, 1, 0)
    level = lax.broadcasted_iota(jnp.int32, falling.shape, 0)
    from_above = jnp.where(level == 0, above, rolled)
    liquid_phase = warm | mixed

    def choose(first, second, last):
        return jnp.where(warm, first, jnp.where(mixed, second, last))

    change = freeze - melting
    zero = jnp.zeros_like(change)
    d_temp = choose(-0.8 * evapor, 0.5 * change, 0.5 * freeze)
    d_vapour = jnp.where(warm, evapor, 0.0)
    d_liquid = -choose(autoconv, freeze + autoconv, freeze)
    d_rain = choose(autoconv - evapor, autoconv + melting, aggreg) + from_above - falling
    d_ice = choose(zero, change, freeze - aggreg)
    after = tuple(
        value + 0.5 * delta
        for value, delta in zip(fields, (d_temp, d_vapour, d_liquid, d_rain, d_ice))
    )
    factor = jnp.where(liquid_phase, 0.4, 0.35) * jnp.tanh(
        vapour - jnp.where(liquid_phase, 1.0, 0.8) * satur
    )
    return after, factor, excess, rolled


def micro_cloud(after, factor, excess, third, icy):
    temper, raw_v, raw_c, raw_r, raw_i = after
    change = 0.5 * factor * (0.5 + sigmoid(third + excess))
    return (
        temper + jnp.where(icy, 1.0, 0.8) * change,
        raw_v - change,
        raw_c + jnp.where(icy, 0.0, change),
        raw_r,
        raw_i + jnp.where(icy, change, 0.0),
    )


def one_hot_fetch(cfg, owner_col, rank_col):
    rows, stride = cfg["fetch_rows"], cfg["fetch_stride"]
    columns = owner_col.shape[0]
    place = lax.broadcasted_iota(jnp.int32, (columns, cfg["peers"] * stride), 1)
    main_at = owner_col * stride + rank_col
    rest_at = owner_col * stride + cfg["main"] + rank_col % rows
    return jnp.concatenate(
        [(place == main_at).astype(F32), (place == rest_at).astype(F32)], axis=0
    ).astype(BF16)


def gather_moments(cfg, fetched, pick, rank_row):
    levels, rows = cfg["levels"], cfg["fetch_rows"]
    columns = rank_row.shape[1]
    row_in = lax.broadcasted_iota(jnp.int32, fetched.shape, 0) % cfg["fetch_stride"]
    fetched = jnp.where(row_in < cfg["main"] + rows, fetched, 0.0)
    high, low = split(fetched)
    both = jnp.dot(pick, jnp.concatenate([high, low], axis=1), preferred_element_type=F32)
    found = (both[:, :LANE] + both[:, LANE:]).T
    main, rest = found[:, :columns], found[:, columns:]
    size = cfg["fetch_rest"]
    total = jnp.zeros((size, columns), F32)
    for group in range(cfg["cap"] // rows):
        total = total + jnp.where(
            rank_row // rows == group, rest[group * size : (group + 1) * size], 0.0
        )
    third = main[:levels]
    first = jnp.concatenate([main[levels:], total], axis=0)
    return first, third


class Links:
    def __init__(self):
        self.nodes, self.devs = lax.axis_size("node"), lax.axis_size("dev")
        self.node, self.dev = lax.axis_index("node"), lax.axis_index("dev")
        self.me = self.node * self.devs + self.dev

    def coordinates(self, peer):
        return (peer // self.devs, peer % self.devs)


def remote(source, target, sends, receives, step, where):
    return pltpu.make_async_remote_copy(
        src_ref=source,
        dst_ref=target,
        send_sem=sends.at[step],
        recv_sem=receives.at[step],
        device_id=where,
        device_id_type=pl.DeviceIdType.MESH,
    )


def each(start, stop, body):
    def step(index, carry):
        body(index)
        return carry

    lax.fori_loop(start, stop, step, 0)


def step_kernel(cfg, blocks, slot_blocks, *refs):
    (
        state_ref,
        moments_ref,
        owner_row_ref,
        regime_ref,
        weights_in_ref,
        rows_ref,
        cols_ref,
        mixed_ref,
        back_ref,
        ocean_ref,
        x_buf,
        m_buf,
        weights_ref,
        early_ref,
        pick_ref,
        put_ref,
        put_rest_ref,
        packed_ref,
        fetched_ref,
        out_ref,
        plane_ref,
        plane_in_ref,
        column_ref,
        a_ref,
        y_buf,
        ratio_ref,
        kappa_ref,
        energy_ref,
        third_ref,
        grad_ref,
        fetch_send,
        fetch_recv,
        back_send,
        back_recv,
        plane_send,
        plane_recv,
        column_send,
        column_recv,
        own_sem,
        own_ocean_sem,
        x_sem,
        m_sem,
        weights_sem,
        mixed_sem,
    ) = refs
    levels = cfg["levels"]

    def block_copies(source, target, sems, count):
        return [
            pltpu.make_async_copy(
                source.at[:, :, pl.ds(block * LANE, LANE)], target.at[block], sems.at[block]
            )
            for block in range(count)
        ]

    m_copies = block_copies(moments_ref, m_buf, m_sem, slot_blocks)
    x_copies = block_copies(state_ref, x_buf, x_sem, blocks)
    weights_copy = pltpu.make_async_copy(weights_in_ref, weights_ref, weights_sem)
    for copy in m_copies + x_copies + [weights_copy]:
        copy.start()
    links = Links()
    me = links.me
    barrier = pltpu.get_barrier_semaphore()
    all_peers = cfg["peers"]

    def greet(step):
        pl.semaphore_signal(
            barrier,
            inc=1,
            device_id=links.coordinates((me + step) % all_peers),
            device_id_type=pl.DeviceIdType.MESH,
        )

    each(1, all_peers, greet)
    for copy in m_copies:
        copy.wait()
    flat_moments = m_buf.reshape(slot_blocks * levels * SUB, LANE)
    pack(cfg, blocks_of(flat_moments, slot_blocks), packed_ref)
    pl.semaphore_wait(barrier, all_peers - 1)

    def fetch_copy(step):
        peer = (me + step) % all_peers
        count = cfg["main"] + cfg["fetch_rows"]
        return remote(
            packed_ref.at[pl.ds(peer * cfg["fetch_stride"], count), :],
            fetched_ref.at[pl.ds(me * cfg["fetch_stride"], count), :],
            fetch_send,
            fetch_recv,
            step,
            links.coordinates(peer),
        )

    each(1, all_peers, lambda step: fetch_copy(step).start())
    own = pl.ds(pl.multiple_of(me * cfg["fetch_stride"], SUB), cfg["fetch_stride"])
    fetched_ref[own, :] = packed_ref[own, :]

    levels, peers, cap = cfg["levels"], cfg["peers"], cfg["cap"]
    columns = blocks * LANE
    x_ref = blocks_of(x_buf.reshape(blocks * levels * SUB, LANE), blocks)
    y_ref = blocks_of(y_buf.reshape(blocks * (levels + 1) * SUB, LANE), blocks)
    a_ref, ratio_ref = blocks_of(a_ref, blocks), blocks_of(ratio_ref, blocks)

    def as_column(row):
        wide = jnp.broadcast_to(row.astype(F32), (LANE, columns)).T
        return wide[:, :1].astype(jnp.int32)

    owner_row = owner_row_ref[...]
    owner_col = as_column(owner_row)
    same = owner_col == owner_row
    down = lax.broadcasted_iota(jnp.int32, (columns, columns), 0)
    across = lax.broadcasted_iota(jnp.int32, (columns, columns), 1)
    rank_row = jnp.sum((same & (down < across)).astype(F32), axis=0, keepdims=True).astype(jnp.int32)
    rank_col = as_column(rank_row)
    pick_ref[...] = one_hot_fetch(cfg, owner_col, rank_col)
    main, rows = cfg["main"], cfg["back_rows"]
    down = lax.broadcasted_iota(jnp.int32, (peers * main, columns), 0)
    put_ref[...] = (down == owner_row * main + rank_row).astype(F32).astype(BF16)
    down = lax.broadcasted_iota(jnp.int32, (peers * SUB, columns), 0)
    put_rest_ref[...] = (down == owner_row * SUB + rank_row % rows).astype(F32).astype(BF16)

    warm = regime_ref[...] == 0
    mixed = regime_ref[...] == 1
    icy = regime_ref[...] == 2
    for copy in x_copies:
        copy.wait()

    def tile_rows(tile, plane):
        return pl.ds(pl.multiple_of(plane * levels + tile * SUB, SUB), SUB)

    def micro_early(tile, above):
        base = tile * (SUB * SUB)
        fields = tuple(read_plane(x_ref, base + field, SUB, SUB) for field in range(5))
        after, factor, excess, rolled = micro_rates(fields, above, warm, mixed)
        for plane, value in enumerate(after + (factor, excess)):
            early_ref[tile_rows(tile, plane), :] = value
        for field in (5, 6, 7):
            value = read_plane(x_ref, base + field, SUB, SUB)
            write_plane(a_ref, base + field, SUB, value)
            write_plane(y_ref, base + field, SUB, value)
        return rolled

    nothing = jnp.zeros((SUB, columns), F32)
    lax.fori_loop(0, levels // SUB, micro_early, nothing)
    pad = pl.ds(levels * SUB, SUB)
    write_tile(y_ref, pad, nothing)
    weights_copy.wait()

    each(1, all_peers, lambda step: fetch_copy(step).wait_recv())
    first, third = gather_moments(cfg, fetched_ref[...], pick_ref[...], rank_row)
    third_ref[...] = third
    below = jnp.concatenate([first[1:], first[-1:]], axis=0)
    energy_ref[...] = 0.5 + 60.0 * sigmoid(2.0 * (first + below))

    def micro(tile, carry):
        base = tile * (SUB * SUB)
        early = tuple(early_ref[tile_rows(tile, plane), :] for plane in range(7))
        moment = third_ref[tile_rows(tile, 0), :]
        fields = micro_cloud(early[:5], early[5], early[6], moment, icy)
        below = []
        for above in carry:
            after, factor, excess, rolled = micro_rates(fields, above, warm, mixed)
            fields = micro_cloud(after, factor, excess, moment, icy)
            below.append(rolled)
        for field in range(5):
            write_plane(a_ref, base + field, SUB, fields[field])
            write_plane(y_ref, base + field, SUB, fields[field])
        return tuple(below)

    lax.fori_loop(0, levels // SUB, micro, (nothing,) * (MICRO_SUB - 1))

    def again(_, carry):
        kappa_tiles(cfg, y_ref, energy_ref, kappa_ref)
        solve(cfg, a_ref, kappa_ref, ratio_ref, y_ref)
        return carry

    lax.fori_loop(0, TURB_ITERS, again, 0)

    last = pl.ds((levels - 1) * SUB, SUB)
    bottom, bottom_a = read_tile(y_ref, last), read_tile(a_ref, last)
    wind = jnp.sqrt(1.0 + bottom[5:6] * bottom[5:6] + bottom[6:7] * bottom[6:7])
    fluxes = jnp.concatenate(
        [
            -0.5 * wind * bottom[5:6],
            -0.5 * wind * bottom[6:7],
            0.5 * softplus(bottom_a[3:4]),
            -0.3 * wind * bottom[0:1],
        ],
        axis=0,
    )
    flux_high = fluxes.astype(BF16).astype(F32)
    doubled = jnp.concatenate([flux_high, fluxes - flux_high], axis=0)
    products = []
    for block in range(weights_ref.shape[0]):
        chosen = jnp.zeros((SUB, LANE), F32)
        for part in range(columns // LANE):
            chosen = jnp.where(
                cols_ref[block] == part, doubled[:, part * LANE : (part + 1) * LANE], chosen
            )
        high, low = split(weights_ref[block])
        wide = jnp.dot(
            chosen.astype(BF16), jnp.concatenate([high, low], axis=1), preferred_element_type=F32
        )
        once = wide[:, :LANE] + wide[:, LANE:]
        once = once + pltpu.roll(once, FLUX, 0)
        products.append(once)
    row_in = lax.broadcasted_iota(jnp.int32, (SUB, LANE), 0) // FLUX
    per_tile = SUB // FLUX
    share = OBLK_DEV * FLUX
    floors = links.devs // 2
    floor, side = links.dev // 2, links.dev % 2
    group = links.nodes * 2
    here = links.node * 2 + side
    span = floors * share
    for member in range(group):
        for level in range(floors):
            owner = member // 2 * links.devs + level * 2 + member % 2
            for part in range(OBLK_DEV // per_tile):
                target = row_in + (owner * OBLK_DEV + part * per_tile)
                total = jnp.zeros((SUB, LANE), F32)
                for block, product in enumerate(products):
                    total = total + jnp.where(target == rows_ref[block], product, 0.0)
                plane_ref[pl.ds(member * span + level * share + part * SUB, SUB), :] = total

    def plane_copy(step):
        member = (here + step) % group
        return remote(
            plane_ref.at[pl.ds(member * span, span), :],
            plane_in_ref.at[pl.ds(here * span, span), :],
            plane_send,
            plane_recv,
            step,
            (member // 2, floor * 2 + member % 2),
        )

    each(1, group, lambda step: plane_copy(step).start())
    mine = pl.ds(pl.multiple_of(here * span, SUB), span)
    plane_in_ref[mine, :] = plane_ref[mine, :]

    live = lax.broadcasted_iota(jnp.int32, (SUB, columns), 0) == SUB - 1
    for index, field in enumerate(GRAD_FIELDS):
        for tile in range(levels // SUB):
            at = tile * SUB * SUB + field
            drop = read_plane(y_ref, at, SUB, SUB) - read_plane(y_ref, at + SUB, SUB, SUB)
            if tile == levels // SUB - 1:
                ends = 1.0 if index == len(GRAD_FIELDS) - 1 else 0.0
                drop = jnp.where(live, ends, drop)
            grad_ref[pl.ds(index * levels + tile * SUB, SUB), :] = drop
    turn = (((1,), (1,)), ((), ()))

    def place(onehot, values):
        high, low = split(values)
        both = lax.dot_general(
            onehot, jnp.concatenate([high, low], axis=0), turn, preferred_element_type=F32
        )
        return both[:, :LANE] + both[:, LANE:]

    size = cfg["back_rest"]
    tail = grad_ref[pl.ds(2 * LANE, size), :]
    groups = cap // rows
    spread = jnp.concatenate(
        [jnp.where(rank_row // rows == group, tail, 0.0) for group in range(groups)], axis=0
    )
    sent = [
        (place(put_ref[...], grad_ref[pl.ds(0, LANE), :]), 0, main),
        (place(put_ref[...], grad_ref[pl.ds(LANE, LANE), :]), main, main),
        (place(put_rest_ref[...], spread), 2 * main, SUB),
    ]
    for value, at, count in sent:
        for peer in range(peers):
            out_ref[pl.ds(peer * cfg["back_stride"] + at, count), :] = value[
                peer * count : (peer + 1) * count
            ]

    def back_copy(step):
        peer = (me + step) % all_peers
        count = 2 * main + rows
        return remote(
            out_ref.at[pl.ds(peer * cfg["back_stride"], count), :],
            back_ref.at[pl.ds(me * cfg["back_stride"], count), :],
            back_send,
            back_recv,
            step,
            links.coordinates(peer),
        )

    each(1, all_peers, lambda step: back_copy(step).start())
    own = pl.ds(pl.multiple_of(me * cfg["back_stride"], SUB), cfg["back_stride"])
    own_copy = pltpu.make_async_copy(out_ref.at[own, :], back_ref.at[own, :], own_sem)
    own_copy.start()

    each(1, group, lambda step: plane_copy(step).wait_recv())
    total = plane_in_ref[pl.ds(0, span), :]
    for member in range(1, group):
        total = total + plane_in_ref[pl.ds(member * span, span), :]
    column_ref[...] = total

    def column_copy(step):
        level = (floor + step) % floors
        return remote(
            column_ref.at[pl.ds(level * share, share), :],
            ocean_ref.at[pl.ds(floor * share, share), :],
            column_send,
            column_recv,
            step,
            (links.node, level * 2 + side),
        )

    each(1, floors, lambda step: column_copy(step).start())
    mine = pl.ds(pl.multiple_of(floor * share, SUB), share)
    own_ocean = pltpu.make_async_copy(column_ref.at[mine, :], ocean_ref.at[mine, :], own_ocean_sem)
    own_ocean.start()

    for field in (2, 3, 4):
        for tile in range(levels // SUB):
            at = tile * SUB * SUB + field
            write_plane(y_ref, at, SUB, read_plane(a_ref, at, SUB, SUB))
    mixed_copies = [
        pltpu.make_async_copy(
            y_buf.at[block, pl.ds(0, levels)],
            mixed_ref.at[:, :, pl.ds(block * LANE, LANE)],
            mixed_sem.at[block],
        )
        for block in range(blocks)
    ]
    for copy in mixed_copies:
        copy.start()

    for copy in mixed_copies:
        copy.wait()
    own_copy.wait()
    own_ocean.wait()
    each(1, all_peers, lambda step: fetch_copy(step).wait_send())
    each(1, group, lambda step: plane_copy(step).wait_send())
    each(1, floors, lambda step: column_copy(step).wait())
    each(1, all_peers, lambda step: back_copy(step).wait())


def update_kernel(
    cfg, moments_ref, state_ref, mixed_ref, back_ref, parts_ref, out_ref, tend_ref, ocean_ref, diff_ref
):
    levels, peers, cap = cfg["levels"], cfg["peers"], cfg["cap"]
    stride, main = cfg["back_stride"], cfg["main"]
    count = len(GRAD_FIELDS) * levels
    block = pl.program_id(0)
    tend_ref[...] = mixed_ref[...] - state_ref[...]

    @pl.when(block == 0)
    def _():
        share = OBLK_DEV * FLUX
        total = parts_ref[pl.ds(0, share), :]
        for floor in range(1, parts_ref.shape[0] // share):
            total = total + parts_ref[pl.ds(floor * share, share), :]
        ocean_ref[...] = total

    width = LANE // peers
    for part in range(2):
        rows = [
            back_ref[pl.ds(part * main + block * width + slot, peers, stride=stride), :]
            for slot in range(width)
        ]
        diff_ref[pl.ds(SUB + part * LANE, LANE), :] = jnp.concatenate(rows, axis=0).T
    rows, size = cfg["back_rows"], cfg["back_rest"]
    turned = jnp.concatenate(
        [back_ref[pl.ds(2 * main + row, peers, stride=stride), :] for row in range(rows)], axis=0
    ).T
    tail = jnp.zeros((size, LANE), F32)
    for group in range(cap // rows):
        tail = jnp.where(block == group, turned[group * size : (group + 1) * size], tail)
    diff_ref[pl.ds(SUB + 2 * LANE, size), :] = tail
    diff_ref[pl.ds(0, SUB), :] = jnp.zeros((SUB, LANE), F32)

    m_ref = [moments_ref.reshape(levels * SUB, LANE)]
    o_ref = [out_ref.reshape(levels * SUB, LANE)]
    live = diff_ref[pl.ds(SUB + count - 1, 1), :] > 0.5
    row_in = lax.broadcasted_iota(jnp.int32, (SUB, LANE), 0)
    for tile in range(levels // SUB):
        grads = []
        for index in range(len(GRAD_FIELDS)):
            at = SUB + index * levels + tile * SUB
            here = diff_ref[pl.ds(at, SUB), :]
            if index == len(GRAD_FIELDS) - 1 and tile == levels // SUB - 1:
                here = jnp.where(row_in == SUB - 1, 0.0, here)
            grads.append(here + diff_ref[pl.ds(at - 1, SUB), :])
        grad_u, grad_v, grad_t, grad_q = grads
        production = [
            grad_u * grad_u + grad_v * grad_v,
            grad_t * grad_t,
            grad_q * grad_q,
            grad_t * grad_q,
            grad_u * grad_t,
            grad_v * grad_t,
            grad_u * grad_q,
            grad_u * grad_v,
        ]
        for index, value in enumerate(production):
            at = tile * SUB * SUB + index
            held = read_plane(m_ref, at, SUB, SUB)
            new = held + 0.5 * (jnp.tanh(value) - (0.3 + 0.1 * index) * held)
            write_plane(o_ref, at, SUB, jnp.where(live, new, held))


VMEM = pl.BlockSpec(memory_space=pltpu.VMEM)
SMEM = pl.BlockSpec(memory_space=pltpu.SMEM)


def local(state, span_owner, regime, moments, remap_weights, remap_rows, remap_cols):
    peers = lax.axis_size("node") * lax.axis_size("dev")
    levels, fields, columns = state.shape
    slots = moments.shape[2]
    blocks = columns // LANE
    cfg = plan(peers, slots // peers, levels)
    params = pltpu.CompilerParams(vmem_limit_bytes=VMEM_BYTES)

    floors = lax.axis_size("dev") // 2
    group = 2 * lax.axis_size("node")
    share = OBLK_DEV * FLUX
    whole = pl.BlockSpec(memory_space=pl.ANY)

    def rows_of(count):
        return pltpu.VMEM((count, LANE), F32)

    def copies_of(count):
        return [pltpu.SemaphoreType.DMA((count,))] * 2

    mixed, back, parts = pl.pallas_call(
        functools.partial(step_kernel, cfg, blocks, slots // LANE),
        out_shape=(
            jax.ShapeDtypeStruct(state.shape, F32),
            jax.ShapeDtypeStruct((peers * cfg["back_stride"], LANE), F32),
            jax.ShapeDtypeStruct((floors * share, LANE), F32),
        ),
        in_specs=[whole, whole, VMEM, VMEM, whole, SMEM, SMEM],
        out_specs=(whole, whole, whole),
        scratch_shapes=[
            pltpu.VMEM((blocks, levels, fields, LANE), F32),
            pltpu.VMEM((slots // LANE, levels, fields, LANE), F32),
            pltpu.VMEM(remap_weights.shape, F32),
            pltpu.VMEM((7 * levels, columns), F32),
            pltpu.VMEM((2 * columns, peers * cfg["fetch_stride"]), BF16),
            pltpu.VMEM((peers * cfg["main"], columns), BF16),
            pltpu.VMEM((peers * SUB, columns), BF16),
            rows_of(peers * cfg["fetch_stride"]),
            rows_of(peers * cfg["fetch_stride"]),
            rows_of(peers * cfg["back_stride"]),
            rows_of(group * floors * share),
            rows_of(group * floors * share),
            rows_of(floors * share),
            rows_of(blocks * levels * fields),
            pltpu.VMEM((blocks, levels + 1, fields, LANE), F32),
            rows_of(blocks * levels * fields),
            pltpu.VMEM((levels, columns), F32),
            pltpu.VMEM((levels, columns), F32),
            pltpu.VMEM((levels, columns), F32),
            pltpu.VMEM((len(GRAD_FIELDS) * levels, columns), F32),
        ]
        + copies_of(peers)
        + copies_of(peers)
        + copies_of(group)
        + copies_of(floors)
        + [pltpu.SemaphoreType.DMA, pltpu.SemaphoreType.DMA]
        + [
            pltpu.SemaphoreType.DMA((blocks,)),
            pltpu.SemaphoreType.DMA((slots // LANE,)),
            pltpu.SemaphoreType.DMA,
            pltpu.SemaphoreType.DMA((blocks,)),
        ],
        compiler_params=pltpu.CompilerParams(
            vmem_limit_bytes=VMEM_BYTES, collective_id=0, has_side_effects=True
        ),
    )(
        state,
        moments,
        span_owner.reshape(1, columns),
        regime.reshape(1, columns),
        remap_weights,
        remap_rows,
        remap_cols,
    )
    steps = slots // LANE
    by_level = pl.BlockSpec((levels // steps, fields, columns), lambda block: (block, 0, 0))
    by_slot = pl.BlockSpec((levels, fields, LANE), lambda block: (0, 0, block))
    moments_out, tendencies, ocean = pl.pallas_call(
        functools.partial(update_kernel, cfg),
        out_shape=(
            jax.ShapeDtypeStruct(moments.shape, F32),
            jax.ShapeDtypeStruct(state.shape, F32),
            jax.ShapeDtypeStruct((OBLK_DEV * FLUX, LANE), F32),
        ),
        grid=(steps,),
        in_specs=[by_slot, by_level, by_level, VMEM, VMEM],
        out_specs=(by_slot, by_level, VMEM),
        scratch_shapes=[pltpu.VMEM((SUB + len(GRAD_FIELDS) * levels, LANE), F32)],
        compiler_params=params,
    )(moments, state, mixed, back, parts)
    return (tendencies, moments_out, ocean.reshape(OBLK_DEV, FLUX, LANE))


def solution(mesh):
    return jax.shard_map(
        local,
        mesh=mesh,
        in_specs=(
            P(None, None, ("node", "dev")),
            P(("node", "dev"), None),
            P(("node", "dev")),
            P(None, None, ("node", "dev")),
            P(("node", "dev"), None, None),
            P(("node", "dev")),
            P(("node", "dev")),
        ),
        out_specs=(
            P(None, None, ("node", "dev")),
            P(None, None, ("node", "dev")),
            P(("node", "dev"), None, None),
        ),
        check_vma=False,
    )
```

```python
import functools

import jax
import jax.numpy as jnp
from jax import lax
from jax.experimental import pallas as pl
from jax.experimental.pallas import tpu as pltpu
from jax.sharding import PartitionSpec as P

MICRO_SUB = 2
TURB_ITERS = 3
OBLK_DEV = 4
LANE = 128
SUB = 8
FLUX = 4
VMEM_BYTES = 60 * 1024 * 1024
GRAD_FIELDS = (5, 6, 0, 1)
F32 = jnp.float32
BF16 = jnp.bfloat16


def plan(peers, cap, levels):
    fetch_rest = 2 * levels - LANE
    back_rest = len(GRAD_FIELDS) * levels - 2 * LANE
    main = max(SUB, cap)
    fetch_rows = max(1, cap * fetch_rest // LANE)
    back_rows = max(1, cap * back_rest // LANE)
    return dict(
        peers=peers,
        cap=cap,
        levels=levels,
        main=main,
        fetch_rest=fetch_rest,
        back_rest=back_rest,
        fetch_rows=fetch_rows,
        back_rows=back_rows,
        fetch_stride=main + SUB,
        back_stride=2 * main + SUB,
    )


def sigmoid(x):
    return 0.5 * jnp.tanh(0.5 * x) + 0.5


def softplus(x):
    return jnp.maximum(x, 0.0) + jnp.log(1.0 + jnp.exp(-jnp.abs(x)))


def inverse(x):
    first = pl.reciprocal(x, approx=True)
    return first * (2.0 - x * first)


def split(x):
    high = x.astype(BF16)
    return high, (x - high.astype(F32)).astype(BF16)


def blocks_of(ref, count):
    rows = ref.shape[0] // count
    return [ref.at[pl.ds(block * rows, rows), :] for block in range(count)]


def read_plane(refs, start, rows, stride):
    return jnp.concatenate([ref[pl.ds(start, rows, stride=stride), :] for ref in refs], axis=1)


def write_plane(refs, start, stride, value):
    for block, ref in enumerate(refs):
        ref[pl.ds(start, value.shape[0], stride=stride), :] = value[
            :, block * LANE : (block + 1) * LANE
        ]


def read_tile(refs, cut):
    return jnp.concatenate([ref[cut, :] for ref in refs], axis=1)


def write_tile(refs, cut, value):
    for block, ref in enumerate(refs):
        ref[cut, :] = value[:, block * LANE : (block + 1) * LANE]


def pack(cfg, flat, out_ref):
    levels, peers, cap = cfg["levels"], cfg["peers"], cfg["cap"]
    stride = cfg["fetch_stride"]
    first = read_plane(flat, 0, levels, SUB)
    third = read_plane(flat, 2, levels, SUB)
    cut = LANE - levels
    main = jnp.concatenate([third, first[:cut]], axis=0).T
    rest = first[cut:]
    for slot in range(cap):
        out_ref[pl.ds(slot, peers, stride=stride), :] = main[slot * peers : (slot + 1) * peers]
    rows = cfg["fetch_rows"]
    groups = cap // rows
    width = rows * peers
    stacked = jnp.concatenate(
        [rest[:, group * width : (group + 1) * width] for group in range(groups)], axis=0
    )
    if stacked.shape[0] < LANE:
        stacked = jnp.concatenate(
            [stacked, jnp.zeros((LANE - stacked.shape[0], width), F32)], axis=0
        )
    if width < LANE:
        stacked = jnp.concatenate([stacked, jnp.zeros((LANE, LANE - width), F32)], axis=1)
    turned = stacked.T
    blank = jnp.zeros((peers, LANE), F32)
    for row in range(cap, cfg["main"]):
        out_ref[pl.ds(row, peers, stride=stride), :] = blank
    for row in range(SUB):
        value = turned[row * peers : (row + 1) * peers] if row < rows else blank
        out_ref[pl.ds(cfg["main"] + row, peers, stride=stride), :] = value


def kappa_tiles(cfg, y_ref, energy_ref, kappa_ref):
    levels = cfg["levels"]
    for tile in range(levels // SUB):
        rows = pl.ds(tile * SUB, SUB)
        here = tile * SUB * SUB

        def drop(field):
            return read_plane(y_ref, here + field, SUB, SUB) - read_plane(
                y_ref, here + SUB + field, SUB, SUB
            )

        diff_u, diff_v, diff_t = drop(5), drop(6), drop(0)
        shear = diff_u * diff_u + diff_v * diff_v
        kappa = (0.3 + 1.5 * shear * inverse(1.0 + shear) * sigmoid(-2.0 * diff_t)) * energy_ref[
            rows, :
        ]
        if tile == levels // SUB - 1:
            level = lax.broadcasted_iota(jnp.int32, kappa.shape, 0)
            kappa = jnp.where(level == SUB - 1, 0.0, kappa)
        kappa_ref[rows, :] = kappa


def solve(cfg, a_ref, kappa_ref, ratio_ref, y_ref):
    levels = cfg["levels"]
    half = levels // 2
    columns = kappa_ref.shape[1]
    zero = jnp.zeros((SUB, columns), F32)

    def tile(level):
        return pl.ds(level * SUB, SUB)

    def kappa_row(level):
        return jnp.broadcast_to(kappa_ref[pl.ds(level, 1), :], (SUB, columns))

    state_of = {0: (zero, zero, zero), 1: (zero, zero, zero)}
    for step in range(half):
        for side in (0, 1):
            level = step if side == 0 else levels - 1 - step
            k_behind, ratio, value = state_of[side]
            k_ahead = kappa_row(level if side == 0 else level - 1)
            scale = inverse((1.0 + k_behind + k_ahead) - k_behind * ratio)
            value = (read_tile(a_ref, tile(level)) + k_behind * value) * scale
            ratio = k_ahead * scale
            write_tile(ratio_ref, tile(level), ratio)
            write_tile(y_ref, tile(level), value)
            state_of[side] = (k_ahead, ratio, value)
    _, ratio_up, value_up = state_of[0]
    _, ratio_low, value_low = state_of[1]
    scale = inverse(1.0 - ratio_up * ratio_low)
    upper = (value_up + ratio_up * value_low) * scale
    lower = (value_low + ratio_low * value_up) * scale
    write_tile(y_ref, tile(half - 1), upper)
    write_tile(y_ref, tile(half), lower)
    for step in range(1, half):
        level = half - 1 - step
        upper = read_tile(y_ref, tile(level)) + read_tile(ratio_ref, tile(level)) * upper
        write_tile(y_ref, tile(level), upper)
        level = half + step
        lower = read_tile(y_ref, tile(level)) + read_tile(ratio_ref, tile(level)) * lower
        write_tile(y_ref, tile(level), lower)


def micro_rates(fields, above, warm, mixed):
    temper, raw_v, raw_c, raw_r, raw_i = fields
    vapour, liquid, rain_q, ice_q = (softplus(raw) for raw in (raw_v, raw_c, raw_r, raw_i))
    satur = 0.6 * jnp.exp(0.5 * jnp.tanh(0.5 * temper))
    excess = vapour - satur
    autoconv = 0.3 * liquid * liquid * inverse(1.0 + liquid)
    evapor = 0.1 * rain_q * sigmoid(-excess)
    warmth = sigmoid(temper)
    freeze = 0.3 * liquid * (1.0 - warmth)
    melting = 0.2 * ice_q * warmth
    aggreg = 0.25 * ice_q * ice_q * inverse(1.0 + ice_q)
    falling = 0.5 * rain_q
    rolled = pltpu.roll(falling, 1, 0)
    level = lax.broadcasted_iota(jnp.int32, falling.shape, 0)
    from_above = jnp.where(level == 0, above, rolled)
    liquid_phase = warm | mixed

    def choose(first, second, last):
        return jnp.where(warm, first, jnp.where(mixed, second, last))

    change = freeze - melting
    zero = jnp.zeros_like(change)
    d_temp = choose(-0.8 * evapor, 0.5 * change, 0.5 * freeze)
    d_vapour = jnp.where(warm, evapor, 0.0)
    d_liquid = -choose(autoconv, freeze + autoconv, freeze)
    d_rain = choose(autoconv - evapor, autoconv + melting, aggreg) + from_above - falling
    d_ice = choose(zero, change, freeze - aggreg)
    after = tuple(
        value + 0.5 * delta
        for value, delta in zip(fields, (d_temp, d_vapour, d_liquid, d_rain, d_ice))
    )
    factor = jnp.where(liquid_phase, 0.4, 0.35) * jnp.tanh(
        vapour - jnp.where(liquid_phase, 1.0, 0.8) * satur
    )
    return after, factor, excess, rolled


def micro_cloud(after, factor, excess, third, icy):
    temper, raw_v, raw_c, raw_r, raw_i = after
    change = 0.5 * factor * (0.5 + sigmoid(third + excess))
    return (
        temper + jnp.where(icy, 1.0, 0.8) * change,
        raw_v - change,
        raw_c + jnp.where(icy, 0.0, change),
        raw_r,
        raw_i + jnp.where(icy, change, 0.0),
    )


def one_hot_fetch(cfg, owner_col, rank_col):
    rows, stride = cfg["fetch_rows"], cfg["fetch_stride"]
    columns = owner_col.shape[0]
    place = lax.broadcasted_iota(jnp.int32, (columns, cfg["peers"] * stride), 1)
    main_at = owner_col * stride + rank_col
    rest_at = owner_col * stride + cfg["main"] + rank_col % rows
    return jnp.concatenate(
        [(place == main_at).astype(F32), (place == rest_at).astype(F32)], axis=0
    ).astype(BF16)


def gather_moments(cfg, fetched, pick, rank_row):
    levels, rows = cfg["levels"], cfg["fetch_rows"]
    columns = rank_row.shape[1]
    row_in = lax.broadcasted_iota(jnp.int32, fetched.shape, 0) % cfg["fetch_stride"]
    fetched = jnp.where(row_in < cfg["main"] + rows, fetched, 0.0)
    high, low = split(fetched)
    both = jnp.dot(pick, jnp.concatenate([high, low], axis=1), preferred_element_type=F32)
    found = (both[:, :LANE] + both[:, LANE:]).T
    main, rest = found[:, :columns], found[:, columns:]
    size = cfg["fetch_rest"]
    total = jnp.zeros((size, columns), F32)
    for group in range(cfg["cap"] // rows):
        total = total + jnp.where(
            rank_row // rows == group, rest[group * size : (group + 1) * size], 0.0
        )
    third = main[:levels]
    first = jnp.concatenate([main[levels:], total], axis=0)
    return first, third


def update(cfg, m_refs, diff_ref, lanes):
    levels = cfg["levels"]
    count = len(GRAD_FIELDS) * levels
    live = diff_ref[pl.ds(SUB + count - 1, 1), lanes] > 0.5
    row_in = lax.broadcasted_iota(jnp.int32, (SUB, lanes.size), 0)
    for tile in range(levels // SUB):
        grads = []
        for index in range(len(GRAD_FIELDS)):
            at = SUB + index * levels + tile * SUB
            here = diff_ref[pl.ds(at, SUB), lanes]
            if index == len(GRAD_FIELDS) - 1 and tile == levels // SUB - 1:
                here = jnp.where(row_in == SUB - 1, 0.0, here)
            grads.append(here + diff_ref[pl.ds(at - 1, SUB), lanes])
        grad_u, grad_v, grad_t, grad_q = grads
        production = [
            grad_u * grad_u + grad_v * grad_v,
            grad_t * grad_t,
            grad_q * grad_q,
            grad_t * grad_q,
            grad_u * grad_t,
            grad_v * grad_t,
            grad_u * grad_q,
            grad_u * grad_v,
        ]
        for index, value in enumerate(production):
            at = tile * SUB * SUB + index
            held = read_plane(m_refs, at, SUB, SUB)
            new = held + 0.5 * (jnp.tanh(value) - (0.3 + 0.1 * index) * held)
            write_plane(m_refs, at, SUB, jnp.where(live, new, held))


class Links:
    def __init__(self):
        self.nodes, self.devs = lax.axis_size("node"), lax.axis_size("dev")
        self.node, self.dev = lax.axis_index("node"), lax.axis_index("dev")
        self.me = self.node * self.devs + self.dev

    def coordinates(self, peer):
        return (peer // self.devs, peer % self.devs)


def remote(source, target, sends, receives, step, where):
    return pltpu.make_async_remote_copy(
        src_ref=source,
        dst_ref=target,
        send_sem=sends.at[step],
        recv_sem=receives.at[step],
        device_id=where,
        device_id_type=pl.DeviceIdType.MESH,
    )


def each(start, stop, body):
    def step(index, carry):
        body(index)
        return carry

    lax.fori_loop(start, stop, step, 0)


def step_kernel(cfg, blocks, slot_blocks, *refs):
    (
        state_ref,
        moments_ref,
        owner_row_ref,
        regime_ref,
        weights_in_ref,
        rows_ref,
        cols_ref,
        tend_ref,
        new_ref,
        ocean_ref,
        x_buf,
        m_buf,
        weights_ref,
        early_ref,
        pick_ref,
        put_ref,
        put_rest_ref,
        packed_ref,
        fetched_ref,
        out_ref,
        plane_ref,
        plane_in_ref,
        column_ref,
        column_in_ref,
        back_ref,
        diff_ref,
        a_ref,
        y_buf,
        ratio_ref,
        kappa_ref,
        energy_ref,
        third_ref,
        grad_ref,
        fetch_send,
        fetch_recv,
        back_send,
        back_recv,
        plane_send,
        plane_recv,
        column_send,
        column_recv,
        x_sem,
        m_sem,
        weights_sem,
    ) = refs
    levels = cfg["levels"]

    def block_copies(source, target, sems, count):
        return [
            pltpu.make_async_copy(
                source.at[:, :, pl.ds(block * LANE, LANE)], target.at[block], sems.at[block]
            )
            for block in range(count)
        ]

    m_copies = block_copies(moments_ref, m_buf, m_sem, slot_blocks)
    x_copies = block_copies(state_ref, x_buf, x_sem, blocks)
    weights_copy = pltpu.make_async_copy(weights_in_ref, weights_ref, weights_sem)
    for copy in m_copies + x_copies + [weights_copy]:
        copy.start()
    links = Links()
    me = links.me
    barrier = pltpu.get_barrier_semaphore()
    all_peers = cfg["peers"]

    def greet(step):
        pl.semaphore_signal(
            barrier,
            inc=1,
            device_id=links.coordinates((me + step) % all_peers),
            device_id_type=pl.DeviceIdType.MESH,
        )

    each(1, all_peers, greet)
    for copy in m_copies:
        copy.wait()
    flat_moments = m_buf.reshape(slot_blocks * levels * SUB, LANE)
    pack(cfg, blocks_of(flat_moments, slot_blocks), packed_ref)
    pl.semaphore_wait(barrier, all_peers - 1)

    def fetch_copy(step):
        peer = (me + step) % all_peers
        count = cfg["main"] + cfg["fetch_rows"]
        return remote(
            packed_ref.at[pl.ds(peer * cfg["fetch_stride"], count), :],
            fetched_ref.at[pl.ds(me * cfg["fetch_stride"], count), :],
            fetch_send,
            fetch_recv,
            step,
            links.coordinates(peer),
        )

    each(1, all_peers, lambda step: fetch_copy(step).start())
    own = pl.ds(pl.multiple_of(me * cfg["fetch_stride"], SUB), cfg["fetch_stride"])
    fetched_ref[own, :] = packed_ref[own, :]

    levels, peers, cap = cfg["levels"], cfg["peers"], cfg["cap"]
    columns = blocks * LANE
    x_ref = blocks_of(x_buf.reshape(blocks * levels * SUB, LANE), blocks)
    y_ref = blocks_of(y_buf.reshape(blocks * (levels + 1) * SUB, LANE), blocks)
    a_ref, ratio_ref = blocks_of(a_ref, blocks), blocks_of(ratio_ref, blocks)

    def as_column(row):
        wide = jnp.broadcast_to(row.astype(F32), (LANE, columns)).T
        return wide[:, :1].astype(jnp.int32)

    owner_row = owner_row_ref[...]
    owner_col = as_column(owner_row)
    same = owner_col == owner_row
    down = lax.broadcasted_iota(jnp.int32, (columns, columns), 0)
    across = lax.broadcasted_iota(jnp.int32, (columns, columns), 1)
    rank_row = jnp.sum((same & (down < across)).astype(F32), axis=0, keepdims=True).astype(jnp.int32)
    rank_col = as_column(rank_row)
    pick_ref[...] = one_hot_fetch(cfg, owner_col, rank_col)
    main, rows = cfg["main"], cfg["back_rows"]
    down = lax.broadcasted_iota(jnp.int32, (peers * main, columns), 0)
    put_ref[...] = (down == owner_row * main + rank_row).astype(F32).astype(BF16)
    down = lax.broadcasted_iota(jnp.int32, (peers * SUB, columns), 0)
    put_rest_ref[...] = (down == owner_row * SUB + rank_row % rows).astype(F32).astype(BF16)

    warm = regime_ref[...] == 0
    mixed = regime_ref[...] == 1
    icy = regime_ref[...] == 2
    for copy in x_copies:
        copy.wait()

    def tile_rows(tile, plane):
        return pl.ds(pl.multiple_of(plane * levels + tile * SUB, SUB), SUB)

    def micro_early(tile, above):
        base = tile * (SUB * SUB)
        fields = tuple(read_plane(x_ref, base + field, SUB, SUB) for field in range(5))
        after, factor, excess, rolled = micro_rates(fields, above, warm, mixed)
        for plane, value in enumerate(after + (factor, excess)):
            early_ref[tile_rows(tile, plane), :] = value
        for field in (5, 6, 7):
            value = read_plane(x_ref, base + field, SUB, SUB)
            write_plane(a_ref, base + field, SUB, value)
            write_plane(y_ref, base + field, SUB, value)
        return rolled

    nothing = jnp.zeros((SUB, columns), F32)
    lax.fori_loop(0, levels // SUB, micro_early, nothing)
    pad = pl.ds(levels * SUB, SUB)
    write_tile(y_ref, pad, nothing)
    weights_copy.wait()

    each(1, all_peers, lambda step: fetch_copy(step).wait_recv())
    first, third = gather_moments(cfg, fetched_ref[...], pick_ref[...], rank_row)
    third_ref[...] = third
    below = jnp.concatenate([first[1:], first[-1:]], axis=0)
    energy_ref[...] = 0.5 + 60.0 * sigmoid(2.0 * (first + below))

    def micro(tile, carry):
        base = tile * (SUB * SUB)
        early = tuple(early_ref[tile_rows(tile, plane), :] for plane in range(7))
        moment = third_ref[tile_rows(tile, 0), :]
        fields = micro_cloud(early[:5], early[5], early[6], moment, icy)
        below = []
        for above in carry:
            after, factor, excess, rolled = micro_rates(fields, above, warm, mixed)
            fields = micro_cloud(after, factor, excess, moment, icy)
            below.append(rolled)
        for field in range(5):
            write_plane(a_ref, base + field, SUB, fields[field])
            write_plane(y_ref, base + field, SUB, fields[field])
        return tuple(below)

    lax.fori_loop(0, levels // SUB, micro, (nothing,) * (MICRO_SUB - 1))

    def again(_, carry):
        kappa_tiles(cfg, y_ref, energy_ref, kappa_ref)
        solve(cfg, a_ref, kappa_ref, ratio_ref, y_ref)
        return carry

    lax.fori_loop(0, TURB_ITERS, again, 0)

    live = lax.broadcasted_iota(jnp.int32, (SUB, columns), 0) == SUB - 1
    for index, field in enumerate(GRAD_FIELDS):
        for tile in range(levels // SUB):
            at = tile * SUB * SUB + field
            drop = read_plane(y_ref, at, SUB, SUB) - read_plane(y_ref, at + SUB, SUB, SUB)
            if tile == levels // SUB - 1:
                ends = 1.0 if index == len(GRAD_FIELDS) - 1 else 0.0
                drop = jnp.where(live, ends, drop)
            grad_ref[pl.ds(index * levels + tile * SUB, SUB), :] = drop
    turn = (((1,), (1,)), ((), ()))

    def place(onehot, values):
        high, low = split(values)
        both = lax.dot_general(
            onehot, jnp.concatenate([high, low], axis=0), turn, preferred_element_type=F32
        )
        return both[:, :LANE] + both[:, LANE:]

    size = cfg["back_rest"]
    tail = grad_ref[pl.ds(2 * LANE, size), :]
    groups = cap // rows
    spread = jnp.concatenate(
        [jnp.where(rank_row // rows == group, tail, 0.0) for group in range(groups)], axis=0
    )
    rest = place(put_rest_ref[...], spread)
    sent = [
        place(put_ref[...], grad_ref[pl.ds(part * LANE, LANE), :]) for part in range(2)
    ]
    halves = main // SUB
    stride = cfg["back_stride"]

    def offset(half):
        return 0 if half == 0 else 3 * SUB + (half - 1) * 2 * SUB

    for peer in range(peers):
        base = peer * stride
        out_ref[pl.ds(base + 2 * SUB, SUB), :] = rest[peer * SUB : (peer + 1) * SUB]
        for half in range(halves):
            for part, value in enumerate(sent):
                at = peer * main + half * SUB
                out_ref[pl.ds(base + offset(half) + part * SUB, SUB), :] = value[at : at + SUB]

    def back_copy(half, step):
        peer = (me + step) % all_peers
        count = 2 * SUB + (rows if half == 0 else 0)
        return remote(
            out_ref.at[pl.ds(peer * stride + offset(half), count), :],
            back_ref.at[pl.ds(me * stride + offset(half), count), :],
            back_send.at[half],
            back_recv.at[half],
            step,
            links.coordinates(peer),
        )

    each(1, all_peers, lambda step: back_copy(0, step).start())

    last = pl.ds((levels - 1) * SUB, SUB)
    bottom, bottom_a = read_tile(y_ref, last), read_tile(a_ref, last)
    wind = jnp.sqrt(1.0 + bottom[5:6] * bottom[5:6] + bottom[6:7] * bottom[6:7])
    fluxes = jnp.concatenate(
        [
            -0.5 * wind * bottom[5:6],
            -0.5 * wind * bottom[6:7],
            0.5 * softplus(bottom_a[3:4]),
            -0.3 * wind * bottom[0:1],
        ],
        axis=0,
    )
    flux_high = fluxes.astype(BF16).astype(F32)
    doubled = jnp.concatenate([flux_high, fluxes - flux_high], axis=0)
    products = []
    for block in range(weights_ref.shape[0]):
        chosen = jnp.zeros((SUB, LANE), F32)
        for part in range(columns // LANE):
            chosen = jnp.where(
                cols_ref[block] == part, doubled[:, part * LANE : (part + 1) * LANE], chosen
            )
        high, low = split(weights_ref[block])
        wide = jnp.dot(
            chosen.astype(BF16), jnp.concatenate([high, low], axis=1), preferred_element_type=F32
        )
        once = wide[:, :LANE] + wide[:, LANE:]
        once = once + pltpu.roll(once, FLUX, 0)
        products.append(once)
    row_in = lax.broadcasted_iota(jnp.int32, (SUB, LANE), 0) // FLUX
    per_tile = SUB // FLUX
    share = OBLK_DEV * FLUX
    floors = links.devs // 2
    floor, side = links.dev // 2, links.dev % 2
    group = links.nodes * 2
    here = links.node * 2 + side
    span = floors * share
    for member in range(group):
        for level in range(floors):
            owner = member // 2 * links.devs + level * 2 + member % 2
            for part in range(OBLK_DEV // per_tile):
                target = row_in + (owner * OBLK_DEV + part * per_tile)
                total = jnp.zeros((SUB, LANE), F32)
                for block, product in enumerate(products):
                    total = total + jnp.where(target == rows_ref[block], product, 0.0)
                plane_ref[pl.ds(member * span + level * share + part * SUB, SUB), :] = total

    def plane_copy(step):
        member = (here + step) % group
        return remote(
            plane_ref.at[pl.ds(member * span, span), :],
            plane_in_ref.at[pl.ds(here * span, span), :],
            plane_send,
            plane_recv,
            step,
            (member // 2, floor * 2 + member % 2),
        )

    each(1, group, lambda step: plane_copy(step).start())
    mine = pl.ds(pl.multiple_of(here * span, SUB), span)
    plane_in_ref[mine, :] = plane_ref[mine, :]

    for half in range(1, halves):
        each(1, all_peers, lambda step: back_copy(half, step).start())
    own = pl.ds(pl.multiple_of(me * stride, SUB), stride)
    back_ref[own, :] = out_ref[own, :]

    field_in = lax.broadcasted_iota(jnp.int32, (SUB, columns), 0)
    kept = (field_in >= 2) & (field_in < 5)
    for level in range(levels):
        cut = pl.ds(level * SUB, SUB)
        ended = jnp.where(kept, read_tile(a_ref, cut), read_tile(y_ref, cut))
        write_tile(x_ref, cut, ended - read_tile(x_ref, cut))
    tend_copies = [
        pltpu.make_async_copy(
            x_buf.at[block], tend_ref.at[:, :, pl.ds(block * LANE, LANE)], x_sem.at[block]
        )
        for block in range(blocks)
    ]
    for copy in tend_copies:
        copy.start()

    each(1, group, lambda step: plane_copy(step).wait_recv())
    total = plane_in_ref[pl.ds(0, span), :]
    for member in range(1, group):
        total = total + plane_in_ref[pl.ds(member * span, span), :]
    column_ref[...] = total

    def column_copy(step):
        level = (floor + step) % floors
        return remote(
            column_ref.at[pl.ds(level * share, share), :],
            column_in_ref.at[pl.ds(floor * share, share), :],
            column_send,
            column_recv,
            step,
            (links.node, level * 2 + side),
        )

    each(1, floors, lambda step: column_copy(step).start())
    moment_blocks = blocks_of(flat_moments, slot_blocks)
    per_block = LANE // peers
    per_half = slot_blocks // halves
    size, count = cfg["back_rest"], len(GRAD_FIELDS) * levels
    out_copies = []
    for half in range(halves):
        each(1, all_peers, lambda step: back_copy(half, step).wait_recv())
        if half == 0:
            turned = jnp.concatenate(
                [back_ref[pl.ds(2 * SUB + row, peers, stride=stride), :] for row in range(rows)],
                axis=0,
            ).T
        mine = range(half * per_half, (half + 1) * per_half)
        for block in mine:
            lanes = pl.ds(block * LANE, LANE)
            diff_ref[pl.ds(0, SUB), lanes] = jnp.zeros((SUB, LANE), F32)
            for part in range(2):
                start = offset(half) + part * SUB + block * per_block - half * SUB
                picked = [
                    back_ref[pl.ds(start + slot, peers, stride=stride), :]
                    for slot in range(per_block)
                ]
                at = SUB + part * LANE
                diff_ref[pl.ds(at, LANE), lanes] = jnp.concatenate(picked, axis=0).T
            diff_ref[pl.ds(SUB + 2 * LANE, size), lanes] = turned[block * size : (block + 1) * size]
        lanes = pl.ds(half * per_half * LANE, per_half * LANE)
        update(cfg, moment_blocks[mine.start : mine.stop], diff_ref, lanes)
        for block in mine:
            copy = pltpu.make_async_copy(
                m_buf.at[block], new_ref.at[:, :, pl.ds(block * LANE, LANE)], m_sem.at[block]
            )
            copy.start()
            out_copies.append(copy)

    each(1, floors, lambda step: column_copy(step).wait_recv())
    total = column_ref[pl.ds(pl.multiple_of(floor * share, SUB), share), :]
    for step in range(1, floors):
        level = (floor + step) % floors
        total = total + column_in_ref[pl.ds(pl.multiple_of(level * share, SUB), share), :]
    ocean_ref[...] = total

    for copy in tend_copies + out_copies:
        copy.wait()
    each(1, all_peers, lambda step: fetch_copy(step).wait_send())
    each(1, group, lambda step: plane_copy(step).wait_send())
    each(1, floors, lambda step: column_copy(step).wait_send())
    for half in range(halves):
        each(1, all_peers, lambda step: back_copy(half, step).wait_send())


def copy_kernel(pieces, *refs):
    count = len(refs) // 2
    sources, targets, sems = refs[:count], refs[count:-1], refs[-1]
    copies = []
    for source, target in zip(sources, targets):
        size = max(1, source.shape[0] // pieces)
        for start in range(0, source.shape[0], size):
            cut = pl.ds(start, min(size, source.shape[0] - start))
            copies.append(pltpu.make_async_copy(source.at[cut], target.at[cut], sems.at[len(copies)]))
    for copy in copies:
        copy.start()
    for copy in copies:
        copy.wait()


VMEM = pl.BlockSpec(memory_space=pltpu.VMEM)
SMEM = pl.BlockSpec(memory_space=pltpu.SMEM)


def local(state, span_owner, regime, moments, remap_weights, remap_rows, remap_cols):
    peers = lax.axis_size("node") * lax.axis_size("dev")
    levels, fields, columns = state.shape
    slots = moments.shape[2]
    blocks = columns // LANE
    cfg = plan(peers, slots // peers, levels)
    params = pltpu.CompilerParams(vmem_limit_bytes=VMEM_BYTES)

    floors = lax.axis_size("dev") // 2
    group = 2 * lax.axis_size("node")
    share = OBLK_DEV * FLUX
    whole = pl.BlockSpec(memory_space=pl.ANY)

    def rows_of(count):
        return pltpu.VMEM((count, LANE), F32)

    def copies_of(count):
        return [pltpu.SemaphoreType.DMA((count,))] * 2

    results = pl.pallas_call(
        functools.partial(step_kernel, cfg, blocks, slots // LANE),
        out_shape=(
            jax.ShapeDtypeStruct(state.shape, F32),
            jax.ShapeDtypeStruct(moments.shape, F32),
            jax.ShapeDtypeStruct((share, LANE), F32),
        ),
        in_specs=[whole, whole, VMEM, VMEM, whole, SMEM, SMEM],
        out_specs=(whole, whole, VMEM),
        scratch_shapes=[
            pltpu.VMEM((blocks, levels, fields, LANE), F32),
            pltpu.VMEM((slots // LANE, levels, fields, LANE), F32),
            pltpu.VMEM(remap_weights.shape, F32),
            pltpu.VMEM((7 * levels, columns), F32),
            pltpu.VMEM((2 * columns, peers * cfg["fetch_stride"]), BF16),
            pltpu.VMEM((peers * cfg["main"], columns), BF16),
            pltpu.VMEM((peers * SUB, columns), BF16),
            rows_of(peers * cfg["fetch_stride"]),
            rows_of(peers * cfg["fetch_stride"]),
            rows_of(peers * cfg["back_stride"]),
            rows_of(group * floors * share),
            rows_of(group * floors * share),
            rows_of(floors * share),
            rows_of(floors * share),
            rows_of(peers * cfg["back_stride"]),
            pltpu.VMEM((SUB + len(GRAD_FIELDS) * levels, slots), F32),
            rows_of(blocks * levels * fields),
            pltpu.VMEM((blocks, levels + 1, fields, LANE), F32),
            rows_of(blocks * levels * fields),
            pltpu.VMEM((levels, columns), F32),
            pltpu.VMEM((levels, columns), F32),
            pltpu.VMEM((levels, columns), F32),
            pltpu.VMEM((len(GRAD_FIELDS) * levels, columns), F32),
        ]
        + copies_of(peers)
        + [pltpu.SemaphoreType.DMA((cfg["main"] // SUB, peers))] * 2
        + copies_of(group)
        + copies_of(floors)
        + [
            pltpu.SemaphoreType.DMA((blocks,)),
            pltpu.SemaphoreType.DMA((slots // LANE,)),
            pltpu.SemaphoreType.DMA,
        ],
        compiler_params=pltpu.CompilerParams(
            vmem_limit_bytes=VMEM_BYTES, collective_id=0, has_side_effects=True
        ),
    )(
        state,
        moments,
        span_owner.reshape(1, columns),
        regime.reshape(1, columns),
        remap_weights,
        remap_rows,
        remap_cols,
    )
    pieces = 8
    tendencies, moments_out, ocean = pl.pallas_call(
        functools.partial(copy_kernel, pieces),
        out_shape=tuple(jax.ShapeDtypeStruct(result.shape, F32) for result in results),
        in_specs=[whole] * 3,
        out_specs=(whole,) * 3,
        scratch_shapes=[pltpu.SemaphoreType.DMA((3 * pieces + 3,))],
        compiler_params=params,
    )(*results)
    return (tendencies, moments_out, ocean.reshape(OBLK_DEV, FLUX, LANE))


def solution(mesh):
    return jax.shard_map(
        local,
        mesh=mesh,
        in_specs=(
            P(None, None, ("node", "dev")),
            P(("node", "dev"), None),
            P(("node", "dev")),
            P(None, None, ("node", "dev")),
            P(("node", "dev"), None, None),
            P(("node", "dev")),
            P(("node", "dev")),
        ),
        out_specs=(
            P(None, None, ("node", "dev")),
            P(None, None, ("node", "dev")),
            P(("node", "dev"), None, None),
        ),
        check_vma=False,
    )
```

```python
import functools

import jax
import jax.numpy as jnp
from jax import lax
from jax.experimental import pallas as pl
from jax.experimental.pallas import tpu as pltpu
from jax.sharding import PartitionSpec as P

MICRO_SUB = 2
TURB_ITERS = 3
OBLK_DEV = 4
LANE = 128
SUB = 8
FLUX = 4
VMEM_BYTES = 58 * 1024 * 1024
GRAD_FIELDS = (5, 6, 0, 1)
F32 = jnp.float32
BF16 = jnp.bfloat16


def plan(peers, cap, levels):
    fetch_rest = 2 * levels - LANE
    back_rest = len(GRAD_FIELDS) * levels - 2 * LANE
    main = max(SUB, cap)
    fetch_rows = max(1, cap * fetch_rest // LANE)
    back_rows = max(1, cap * back_rest // LANE)
    return dict(
        peers=peers,
        cap=cap,
        levels=levels,
        main=main,
        fetch_rest=fetch_rest,
        back_rest=back_rest,
        fetch_rows=fetch_rows,
        back_rows=back_rows,
        fetch_stride=main + SUB,
        back_stride=2 * main + SUB,
    )


def sigmoid(x):
    return 0.5 * jnp.tanh(0.5 * x) + 0.5


def softplus(x):
    return jnp.maximum(x, 0.0) + jnp.log(1.0 + jnp.exp(-jnp.abs(x)))


def inverse(x):
    first = pl.reciprocal(x, approx=True)
    return first * (2.0 - x * first)


def split(x):
    high = x.astype(BF16)
    return high, (x - high.astype(F32)).astype(BF16)


def blocks_of(ref, count):
    rows = ref.shape[0] // count
    return [ref.at[pl.ds(block * rows, rows), :] for block in range(count)]


def read_plane(refs, start, rows, stride):
    return jnp.concatenate([ref[pl.ds(start, rows, stride=stride), :] for ref in refs], axis=1)


def write_plane(refs, start, stride, value):
    for block, ref in enumerate(refs):
        ref[pl.ds(start, value.shape[0], stride=stride), :] = value[
            :, block * LANE : (block + 1) * LANE
        ]


def read_tile(refs, cut):
    return jnp.concatenate([ref[cut, :] for ref in refs], axis=1)


def write_tile(refs, cut, value):
    for block, ref in enumerate(refs):
        ref[cut, :] = value[:, block * LANE : (block + 1) * LANE]


def pack(cfg, flat, out_ref):
    levels, peers, cap = cfg["levels"], cfg["peers"], cfg["cap"]
    stride = cfg["fetch_stride"]
    first = read_plane(flat, 0, levels, SUB)
    third = read_plane(flat, 2, levels, SUB)
    cut = LANE - levels
    main = jnp.concatenate([third, first[:cut]], axis=0).T
    rest = first[cut:]
    for slot in range(cap):
        out_ref[pl.ds(slot, peers, stride=stride), :] = main[slot * peers : (slot + 1) * peers]
    rows = cfg["fetch_rows"]
    groups = cap // rows
    width = rows * peers
    stacked = jnp.concatenate(
        [rest[:, group * width : (group + 1) * width] for group in range(groups)], axis=0
    )
    if stacked.shape[0] < LANE:
        stacked = jnp.concatenate(
            [stacked, jnp.zeros((LANE - stacked.shape[0], width), F32)], axis=0
        )
    if width < LANE:
        stacked = jnp.concatenate([stacked, jnp.zeros((LANE, LANE - width), F32)], axis=1)
    turned = stacked.T
    blank = jnp.zeros((peers, LANE), F32)
    for row in range(cap, cfg["main"]):
        out_ref[pl.ds(row, peers, stride=stride), :] = blank
    for row in range(SUB):
        value = turned[row * peers : (row + 1) * peers] if row < rows else blank
        out_ref[pl.ds(cfg["main"] + row, peers, stride=stride), :] = value


def kappa_tiles(cfg, y_ref, energy_ref, kappa_ref):
    levels = cfg["levels"]
    for tile in range(levels // SUB):
        rows = pl.ds(tile * SUB, SUB)
        here = tile * SUB * SUB

        def drop(field):
            return read_plane(y_ref, here + field, SUB, SUB) - read_plane(
                y_ref, here + SUB + field, SUB, SUB
            )

        diff_u, diff_v, diff_t = drop(5), drop(6), drop(0)
        shear = diff_u * diff_u + diff_v * diff_v
        kappa = (0.3 + 1.5 * shear * inverse(1.0 + shear) * sigmoid(-2.0 * diff_t)) * energy_ref[
            rows, :
        ]
        if tile == levels // SUB - 1:
            level = lax.broadcasted_iota(jnp.int32, kappa.shape, 0)
            kappa = jnp.where(level == SUB - 1, 0.0, kappa)
        kappa_ref[rows, :] = kappa


def solve(cfg, a_ref, kappa_ref, ratio_ref, y_ref):
    levels = cfg["levels"]
    half = levels // 2
    columns = kappa_ref.shape[1]
    zero = jnp.zeros((SUB, columns), F32)

    def tile(level):
        return pl.ds(level * SUB, SUB)

    def kappa_row(level):
        return jnp.broadcast_to(kappa_ref[pl.ds(level, 1), :], (SUB, columns))

    state_of = {0: (zero, zero, zero), 1: (zero, zero, zero)}
    for step in range(half):
        for side in (0, 1):
            level = step if side == 0 else levels - 1 - step
            k_behind, ratio, value = state_of[side]
            k_ahead = kappa_row(level if side == 0 else level - 1)
            scale = inverse((1.0 + k_behind + k_ahead) - k_behind * ratio)
            value = (read_tile(a_ref, tile(level)) + k_behind * value) * scale
            ratio = k_ahead * scale
            write_tile(ratio_ref, tile(level), ratio)
            write_tile(y_ref, tile(level), value)
            state_of[side] = (k_ahead, ratio, value)
    _, ratio_up, value_up = state_of[0]
    _, ratio_low, value_low = state_of[1]
    scale = inverse(1.0 - ratio_up * ratio_low)
    upper = (value_up + ratio_up * value_low) * scale
    lower = (value_low + ratio_low * value_up) * scale
    write_tile(y_ref, tile(half - 1), upper)
    write_tile(y_ref, tile(half), lower)
    for step in range(1, half):
        level = half - 1 - step
        upper = read_tile(y_ref, tile(level)) + read_tile(ratio_ref, tile(level)) * upper
        write_tile(y_ref, tile(level), upper)
        level = half + step
        lower = read_tile(y_ref, tile(level)) + read_tile(ratio_ref, tile(level)) * lower
        write_tile(y_ref, tile(level), lower)


def micro_rates(fields, above, warm, mixed):
    temper, raw_v, raw_c, raw_r, raw_i = fields
    vapour, liquid, rain_q, ice_q = (softplus(raw) for raw in (raw_v, raw_c, raw_r, raw_i))
    satur = 0.6 * jnp.exp(0.5 * jnp.tanh(0.5 * temper))
    excess = vapour - satur
    autoconv = 0.3 * liquid * liquid * inverse(1.0 + liquid)
    evapor = 0.1 * rain_q * sigmoid(-excess)
    warmth = sigmoid(temper)
    freeze = 0.3 * liquid * (1.0 - warmth)
    melting = 0.2 * ice_q * warmth
    aggreg = 0.25 * ice_q * ice_q * inverse(1.0 + ice_q)
    falling = 0.5 * rain_q
    rolled = pltpu.roll(falling, 1, 0)
    level = lax.broadcasted_iota(jnp.int32, falling.shape, 0)
    from_above = jnp.where(level == 0, above, rolled)
    liquid_phase = warm | mixed

    def choose(first, second, last):
        return jnp.where(warm, first, jnp.where(mixed, second, last))

    change = freeze - melting
    zero = jnp.zeros_like(change)
    d_temp = choose(-0.8 * evapor, 0.5 * change, 0.5 * freeze)
    d_vapour = jnp.where(warm, evapor, 0.0)
    d_liquid = -choose(autoconv, freeze + autoconv, freeze)
    d_rain = choose(autoconv - evapor, autoconv + melting, aggreg) + from_above - falling
    d_ice = choose(zero, change, freeze - aggreg)
    after = tuple(
        value + 0.5 * delta
        for value, delta in zip(fields, (d_temp, d_vapour, d_liquid, d_rain, d_ice))
    )
    factor = jnp.where(liquid_phase, 0.4, 0.35) * jnp.tanh(
        vapour - jnp.where(liquid_phase, 1.0, 0.8) * satur
    )
    return after, factor, excess, rolled


def micro_cloud(after, factor, excess, third, icy):
    temper, raw_v, raw_c, raw_r, raw_i = after
    change = 0.5 * factor * (0.5 + sigmoid(third + excess))
    return (
        temper + jnp.where(icy, 1.0, 0.8) * change,
        raw_v - change,
        raw_c + jnp.where(icy, 0.0, change),
        raw_r,
        raw_i + jnp.where(icy, change, 0.0),
    )


def one_hot_fetch(cfg, owner_col, rank_col):
    rows, stride = cfg["fetch_rows"], cfg["fetch_stride"]
    columns = owner_col.shape[0]
    place = lax.broadcasted_iota(jnp.int32, (columns, cfg["peers"] * stride), 1)
    main_at = owner_col * stride + rank_col
    rest_at = owner_col * stride + cfg["main"] + rank_col % rows
    return jnp.concatenate(
        [(place == main_at).astype(F32), (place == rest_at).astype(F32)], axis=0
    ).astype(BF16)


def gather_moments(cfg, fetched, pick, rank_row):
    levels, rows = cfg["levels"], cfg["fetch_rows"]
    columns = rank_row.shape[1]
    row_in = lax.broadcasted_iota(jnp.int32, fetched.shape, 0) % cfg["fetch_stride"]
    fetched = jnp.where(row_in < cfg["main"] + rows, fetched, 0.0)
    high, low = split(fetched)
    both = jnp.dot(pick, jnp.concatenate([high, low], axis=1), preferred_element_type=F32)
    found = (both[:, :LANE] + both[:, LANE:]).T
    main, rest = found[:, :columns], found[:, columns:]
    size = cfg["fetch_rest"]
    total = jnp.zeros((size, columns), F32)
    for group in range(cfg["cap"] // rows):
        total = total + jnp.where(
            rank_row // rows == group, rest[group * size : (group + 1) * size], 0.0
        )
    third = main[:levels]
    first = jnp.concatenate([main[levels:], total], axis=0)
    return first, third


def update(cfg, m_refs, diff_ref, lanes):
    levels = cfg["levels"]
    count = len(GRAD_FIELDS) * levels
    live = diff_ref[pl.ds(SUB + count - 1, 1), lanes] > 0.5
    row_in = lax.broadcasted_iota(jnp.int32, (SUB, lanes.size), 0)
    for tile in range(levels // SUB):
        grads = []
        for index in range(len(GRAD_FIELDS)):
            at = SUB + index * levels + tile * SUB
            here = diff_ref[pl.ds(at, SUB), lanes]
            if index == len(GRAD_FIELDS) - 1 and tile == levels // SUB - 1:
                here = jnp.where(row_in == SUB - 1, 0.0, here)
            grads.append(here + diff_ref[pl.ds(at - 1, SUB), lanes])
        grad_u, grad_v, grad_t, grad_q = grads
        production = [
            grad_u * grad_u + grad_v * grad_v,
            grad_t * grad_t,
            grad_q * grad_q,
            grad_t * grad_q,
            grad_u * grad_t,
            grad_v * grad_t,
            grad_u * grad_q,
            grad_u * grad_v,
        ]
        for index, value in enumerate(production):
            at = tile * SUB * SUB + index
            held = read_plane(m_refs, at, SUB, SUB)
            new = held + 0.5 * (jnp.tanh(value) - (0.3 + 0.1 * index) * held)
            write_plane(m_refs, at, SUB, jnp.where(live, new, held))


class Links:
    def __init__(self):
        self.nodes, self.devs = lax.axis_size("node"), lax.axis_size("dev")
        self.node, self.dev = lax.axis_index("node"), lax.axis_index("dev")
        self.me = self.node * self.devs + self.dev

    def coordinates(self, peer):
        return (peer // self.devs, peer % self.devs)


def remote(source, target, sends, receives, step, where):
    return pltpu.make_async_remote_copy(
        src_ref=source,
        dst_ref=target,
        send_sem=sends.at[step],
        recv_sem=receives.at[step],
        device_id=where,
        device_id_type=pl.DeviceIdType.MESH,
    )


def each(start, stop, body):
    def step(index, carry):
        body(index)
        return carry

    lax.fori_loop(start, stop, step, 0)


def step_kernel(cfg, blocks, slot_blocks, *refs):
    (
        state_ref,
        moments_ref,
        owner_row_ref,
        regime_ref,
        weights_in_ref,
        rows_ref,
        cols_ref,
        x_buf,
        m_buf,
        ocean_ref,
        weights_ref,
        early_ref,
        pick_ref,
        put_ref,
        put_rest_ref,
        packed_ref,
        fetched_ref,
        out_ref,
        plane_ref,
        plane_in_ref,
        column_ref,
        column_in_ref,
        back_ref,
        diff_ref,
        a_ref,
        y_buf,
        ratio_ref,
        kappa_ref,
        energy_ref,
        third_ref,
        grad_ref,
        fetch_send,
        fetch_recv,
        back_send,
        back_recv,
        plane_send,
        plane_recv,
        column_send,
        column_recv,
        x_sem,
        m_sem,
        weights_sem,
    ) = refs
    levels = cfg["levels"]

    def block_copies(source, target, sems, count):
        return [
            pltpu.make_async_copy(
                source.at[:, :, pl.ds(block * LANE, LANE)], target.at[block], sems.at[block]
            )
            for block in range(count)
        ]

    m_copies = block_copies(moments_ref, m_buf, m_sem, slot_blocks)
    x_copies = block_copies(state_ref, x_buf, x_sem, blocks)
    weights_copy = pltpu.make_async_copy(weights_in_ref, weights_ref, weights_sem)
    for copy in m_copies + x_copies + [weights_copy]:
        copy.start()
    links = Links()
    me = links.me
    barrier = pltpu.get_barrier_semaphore()
    all_peers = cfg["peers"]

    def greet(step):
        pl.semaphore_signal(
            barrier,
            inc=1,
            device_id=links.coordinates((me + step) % all_peers),
            device_id_type=pl.DeviceIdType.MESH,
        )

    each(1, all_peers, greet)
    for copy in m_copies:
        copy.wait()
    flat_moments = m_buf.reshape(slot_blocks * levels * SUB, LANE)
    pack(cfg, blocks_of(flat_moments, slot_blocks), packed_ref)
    pl.semaphore_wait(barrier, all_peers - 1)

    def fetch_copy(step):
        peer = (me + step) % all_peers
        count = cfg["main"] + cfg["fetch_rows"]
        return remote(
            packed_ref.at[pl.ds(peer * cfg["fetch_stride"], count), :],
            fetched_ref.at[pl.ds(me * cfg["fetch_stride"], count), :],
            fetch_send,
            fetch_recv,
            step,
            links.coordinates(peer),
        )

    each(1, all_peers, lambda step: fetch_copy(step).start())
    own = pl.ds(pl.multiple_of(me * cfg["fetch_stride"], SUB), cfg["fetch_stride"])
    fetched_ref[own, :] = packed_ref[own, :]

    levels, peers, cap = cfg["levels"], cfg["peers"], cfg["cap"]
    columns = blocks * LANE
    x_ref = blocks_of(x_buf.reshape(blocks * levels * SUB, LANE), blocks)
    y_ref = blocks_of(y_buf.reshape(blocks * (levels + 1) * SUB, LANE), blocks)
    a_ref, ratio_ref = blocks_of(a_ref, blocks), blocks_of(ratio_ref, blocks)

    def as_column(row):
        wide = jnp.broadcast_to(row.astype(F32), (LANE, columns)).T
        return wide[:, :1].astype(jnp.int32)

    owner_row = owner_row_ref[...]
    owner_col = as_column(owner_row)
    same = owner_col == owner_row
    down = lax.broadcasted_iota(jnp.int32, (columns, columns), 0)
    across = lax.broadcasted_iota(jnp.int32, (columns, columns), 1)
    rank_row = jnp.sum((same & (down < across)).astype(F32), axis=0, keepdims=True).astype(jnp.int32)
    rank_col = as_column(rank_row)
    pick_ref[...] = one_hot_fetch(cfg, owner_col, rank_col)
    main, rows = cfg["main"], cfg["back_rows"]
    down = lax.broadcasted_iota(jnp.int32, (peers * main, columns), 0)
    put_ref[...] = (down == owner_row * main + rank_row).astype(F32).astype(BF16)
    down = lax.broadcasted_iota(jnp.int32, (peers * SUB, columns), 0)
    put_rest_ref[...] = (down == owner_row * SUB + rank_row % rows).astype(F32).astype(BF16)

    warm = regime_ref[...] == 0
    mixed = regime_ref[...] == 1
    icy = regime_ref[...] == 2
    for copy in x_copies:
        copy.wait()

    def tile_rows(tile, plane):
        return pl.ds(pl.multiple_of(plane * levels + tile * SUB, SUB), SUB)

    def micro_early(tile, above):
        base = tile * (SUB * SUB)
        fields = tuple(read_plane(x_ref, base + field, SUB, SUB) for field in range(5))
        after, factor, excess, rolled = micro_rates(fields, above, warm, mixed)
        for plane, value in enumerate(after + (factor, excess)):
            early_ref[tile_rows(tile, plane), :] = value
        for field in (5, 6, 7):
            value = read_plane(x_ref, base + field, SUB, SUB)
            write_plane(a_ref, base + field, SUB, value)
            write_plane(y_ref, base + field, SUB, value)
        return rolled

    nothing = jnp.zeros((SUB, columns), F32)
    lax.fori_loop(0, levels // SUB, micro_early, nothing)
    pad = pl.ds(levels * SUB, SUB)
    write_tile(y_ref, pad, nothing)
    weights_copy.wait()

    each(1, all_peers, lambda step: fetch_copy(step).wait_recv())
    first, third = gather_moments(cfg, fetched_ref[...], pick_ref[...], rank_row)
    third_ref[...] = third
    below = jnp.concatenate([first[1:], first[-1:]], axis=0)
    energy_ref[...] = 0.5 + 60.0 * sigmoid(2.0 * (first + below))

    def micro(tile, carry):
        base = tile * (SUB * SUB)
        early = tuple(early_ref[tile_rows(tile, plane), :] for plane in range(7))
        moment = third_ref[tile_rows(tile, 0), :]
        fields = micro_cloud(early[:5], early[5], early[6], moment, icy)
        below = []
        for above in carry:
            after, factor, excess, rolled = micro_rates(fields, above, warm, mixed)
            fields = micro_cloud(after, factor, excess, moment, icy)
            below.append(rolled)
        for field in range(5):
            write_plane(a_ref, base + field, SUB, fields[field])
            write_plane(y_ref, base + field, SUB, fields[field])
        return tuple(below)

    lax.fori_loop(0, levels // SUB, micro, (nothing,) * (MICRO_SUB - 1))

    def again(_, carry):
        kappa_tiles(cfg, y_ref, energy_ref, kappa_ref)
        solve(cfg, a_ref, kappa_ref, ratio_ref, y_ref)
        return carry

    lax.fori_loop(0, TURB_ITERS, again, 0)

    live = lax.broadcasted_iota(jnp.int32, (SUB, columns), 0) == SUB - 1
    for index, field in enumerate(GRAD_FIELDS):
        for tile in range(levels // SUB):
            at = tile * SUB * SUB + field
            drop = read_plane(y_ref, at, SUB, SUB) - read_plane(y_ref, at + SUB, SUB, SUB)
            if tile == levels // SUB - 1:
                ends = 1.0 if index == len(GRAD_FIELDS) - 1 else 0.0
                drop = jnp.where(live, ends, drop)
            grad_ref[pl.ds(index * levels + tile * SUB, SUB), :] = drop
    turn = (((1,), (1,)), ((), ()))

    def place(onehot, values):
        high, low = split(values)
        both = lax.dot_general(
            onehot, jnp.concatenate([high, low], axis=0), turn, preferred_element_type=F32
        )
        return both[:, :LANE] + both[:, LANE:]

    size = cfg["back_rest"]
    tail = grad_ref[pl.ds(2 * LANE, size), :]
    groups = cap // rows
    spread = jnp.concatenate(
        [jnp.where(rank_row // rows == group, tail, 0.0) for group in range(groups)], axis=0
    )
    rest = place(put_rest_ref[...], spread)
    sent = [
        place(put_ref[...], grad_ref[pl.ds(part * LANE, LANE), :]) for part in range(2)
    ]
    halves = main // SUB
    stride = cfg["back_stride"]

    def offset(half):
        return 0 if half == 0 else 3 * SUB + (half - 1) * 2 * SUB

    for peer in range(peers):
        base = peer * stride
        out_ref[pl.ds(base + 2 * SUB, SUB), :] = rest[peer * SUB : (peer + 1) * SUB]
        for half in range(halves):
            for part, value in enumerate(sent):
                at = peer * main + half * SUB
                out_ref[pl.ds(base + offset(half) + part * SUB, SUB), :] = value[at : at + SUB]

    def back_copy(half, step):
        peer = (me + step) % all_peers
        count = 2 * SUB + (rows if half == 0 else 0)
        return remote(
            out_ref.at[pl.ds(peer * stride + offset(half), count), :],
            back_ref.at[pl.ds(me * stride + offset(half), count), :],
            back_send.at[half],
            back_recv.at[half],
            step,
            links.coordinates(peer),
        )

    each(1, all_peers, lambda step: back_copy(0, step).start())

    last = pl.ds((levels - 1) * SUB, SUB)
    bottom, bottom_a = read_tile(y_ref, last), read_tile(a_ref, last)
    wind = jnp.sqrt(1.0 + bottom[5:6] * bottom[5:6] + bottom[6:7] * bottom[6:7])
    fluxes = jnp.concatenate(
        [
            -0.5 * wind * bottom[5:6],
            -0.5 * wind * bottom[6:7],
            0.5 * softplus(bottom_a[3:4]),
            -0.3 * wind * bottom[0:1],
        ],
        axis=0,
    )
    flux_high = fluxes.astype(BF16).astype(F32)
    doubled = jnp.concatenate([flux_high, fluxes - flux_high], axis=0)
    products = []
    for block in range(weights_ref.shape[0]):
        chosen = jnp.zeros((SUB, LANE), F32)
        for part in range(columns // LANE):
            chosen = jnp.where(
                cols_ref[block] == part, doubled[:, part * LANE : (part + 1) * LANE], chosen
            )
        high, low = split(weights_ref[block])
        wide = jnp.dot(
            chosen.astype(BF16), jnp.concatenate([high, low], axis=1), preferred_element_type=F32
        )
        once = wide[:, :LANE] + wide[:, LANE:]
        once = once + pltpu.roll(once, FLUX, 0)
        products.append(once)
    row_in = lax.broadcasted_iota(jnp.int32, (SUB, LANE), 0) // FLUX
    per_tile = SUB // FLUX
    share = OBLK_DEV * FLUX
    floors = links.devs // 2
    floor, side = links.dev // 2, links.dev % 2
    group = links.nodes * 2
    here = links.node * 2 + side
    span = floors * share
    for member in range(group):
        for level in range(floors):
            owner = member // 2 * links.devs + level * 2 + member % 2
            for part in range(OBLK_DEV // per_tile):
                target = row_in + (owner * OBLK_DEV + part * per_tile)
                total = jnp.zeros((SUB, LANE), F32)
                for block, product in enumerate(products):
                    total = total + jnp.where(target == rows_ref[block], product, 0.0)
                plane_ref[pl.ds(member * span + level * share + part * SUB, SUB), :] = total

    def plane_copy(step):
        member = (here + step) % group
        return remote(
            plane_ref.at[pl.ds(member * span, span), :],
            plane_in_ref.at[pl.ds(here * span, span), :],
            plane_send,
            plane_recv,
            step,
            (member // 2, floor * 2 + member % 2),
        )

    each(1, group, lambda step: plane_copy(step).start())
    mine = pl.ds(pl.multiple_of(here * span, SUB), span)
    plane_in_ref[mine, :] = plane_ref[mine, :]

    for half in range(1, halves):
        each(1, all_peers, lambda step: back_copy(half, step).start())
    own = pl.ds(pl.multiple_of(me * stride, SUB), stride)
    back_ref[own, :] = out_ref[own, :]

    field_in = lax.broadcasted_iota(jnp.int32, (SUB, columns), 0)
    kept = (field_in >= 2) & (field_in < 5)
    for level in range(levels):
        cut = pl.ds(level * SUB, SUB)
        ended = jnp.where(kept, read_tile(a_ref, cut), read_tile(y_ref, cut))
        write_tile(x_ref, cut, ended - read_tile(x_ref, cut))
    each(1, group, lambda step: plane_copy(step).wait_recv())
    total = plane_in_ref[pl.ds(0, span), :]
    for member in range(1, group):
        total = total + plane_in_ref[pl.ds(member * span, span), :]
    column_ref[...] = total

    def column_copy(step):
        level = (floor + step) % floors
        return remote(
            column_ref.at[pl.ds(level * share, share), :],
            column_in_ref.at[pl.ds(floor * share, share), :],
            column_send,
            column_recv,
            step,
            (links.node, level * 2 + side),
        )

    each(1, floors, lambda step: column_copy(step).start())
    moment_blocks = blocks_of(flat_moments, slot_blocks)
    per_block = LANE // peers
    per_half = slot_blocks // halves
    size, count = cfg["back_rest"], len(GRAD_FIELDS) * levels
    for half in range(halves):
        each(1, all_peers, lambda step: back_copy(half, step).wait_recv())
        if half == 0:
            turned = jnp.concatenate(
                [back_ref[pl.ds(2 * SUB + row, peers, stride=stride), :] for row in range(rows)],
                axis=0,
            ).T
        mine = range(half * per_half, (half + 1) * per_half)
        for block in mine:
            lanes = pl.ds(block * LANE, LANE)
            diff_ref[pl.ds(0, SUB), lanes] = jnp.zeros((SUB, LANE), F32)
            for part in range(2):
                start = offset(half) + part * SUB + block * per_block - half * SUB
                picked = [
                    back_ref[pl.ds(start + slot, peers, stride=stride), :]
                    for slot in range(per_block)
                ]
                at = SUB + part * LANE
                diff_ref[pl.ds(at, LANE), lanes] = jnp.concatenate(picked, axis=0).T
            diff_ref[pl.ds(SUB + 2 * LANE, size), lanes] = turned[block * size : (block + 1) * size]
        lanes = pl.ds(half * per_half * LANE, per_half * LANE)
        update(cfg, moment_blocks[mine.start : mine.stop], diff_ref, lanes)

    each(1, floors, lambda step: column_copy(step).wait_recv())
    total = column_ref[pl.ds(pl.multiple_of(floor * share, SUB), share), :]
    for step in range(1, floors):
        level = (floor + step) % floors
        total = total + column_in_ref[pl.ds(pl.multiple_of(level * share, SUB), share), :]
    ocean_ref[...] = total

    each(1, all_peers, lambda step: fetch_copy(step).wait_send())
    each(1, group, lambda step: plane_copy(step).wait_send())
    each(1, floors, lambda step: column_copy(step).wait_send())
    for half in range(halves):
        each(1, all_peers, lambda step: back_copy(half, step).wait_send())


def write_kernel(tend_in_ref, moments_in_ref, ocean_in_ref, tend_ref, moments_ref, ocean_ref, sems):
    copies = [pltpu.make_async_copy(ocean_in_ref, ocean_ref, sems.at[0])]
    for source, target in ((moments_in_ref, moments_ref), (tend_in_ref, tend_ref)):
        for block in range(source.shape[0]):
            place = target.at[:, :, pl.ds(block * LANE, LANE)]
            copies.append(pltpu.make_async_copy(source.at[block], place, sems.at[len(copies)]))
    for copy in copies:
        copy.start()
    for copy in copies:
        copy.wait()


VMEM = pl.BlockSpec(memory_space=pltpu.VMEM)
SMEM = pl.BlockSpec(memory_space=pltpu.SMEM)


def local(state, span_owner, regime, moments, remap_weights, remap_rows, remap_cols):
    peers = lax.axis_size("node") * lax.axis_size("dev")
    levels, fields, columns = state.shape
    slots = moments.shape[2]
    blocks = columns // LANE
    cfg = plan(peers, slots // peers, levels)
    params = pltpu.CompilerParams(vmem_limit_bytes=8 * 1024 * 1024)

    floors = lax.axis_size("dev") // 2
    group = 2 * lax.axis_size("node")
    share = OBLK_DEV * FLUX
    whole = pl.BlockSpec(memory_space=pl.ANY)

    def rows_of(count):
        return pltpu.VMEM((count, LANE), F32)

    def copies_of(count):
        return [pltpu.SemaphoreType.DMA((count,))] * 2

    results = pl.pallas_call(
        functools.partial(step_kernel, cfg, blocks, slots // LANE),
        out_shape=(
            pltpu.VMEM((blocks, levels, fields, LANE), F32),
            pltpu.VMEM((slots // LANE, levels, fields, LANE), F32),
            pltpu.VMEM((share, LANE), F32),
        ),
        in_specs=[whole, whole, VMEM, VMEM, whole, SMEM, SMEM],
        out_specs=(VMEM, VMEM, VMEM),
        scratch_shapes=[
            pltpu.VMEM(remap_weights.shape, F32),
            pltpu.VMEM((7 * levels, columns), F32),
            pltpu.VMEM((2 * columns, peers * cfg["fetch_stride"]), BF16),
            pltpu.VMEM((peers * cfg["main"], columns), BF16),
            pltpu.VMEM((peers * SUB, columns), BF16),
            rows_of(peers * cfg["fetch_stride"]),
            rows_of(peers * cfg["fetch_stride"]),
            rows_of(peers * cfg["back_stride"]),
            rows_of(group * floors * share),
            rows_of(group * floors * share),
            rows_of(floors * share),
            rows_of(floors * share),
            rows_of(peers * cfg["back_stride"]),
            pltpu.VMEM((SUB + len(GRAD_FIELDS) * levels, slots), F32),
            rows_of(blocks * levels * fields),
            pltpu.VMEM((blocks, levels + 1, fields, LANE), F32),
            rows_of(blocks * levels * fields),
            pltpu.VMEM((levels, columns), F32),
            pltpu.VMEM((levels, columns), F32),
            pltpu.VMEM((levels, columns), F32),
            pltpu.VMEM((len(GRAD_FIELDS) * levels, columns), F32),
        ]
        + copies_of(peers)
        + [pltpu.SemaphoreType.DMA((cfg["main"] // SUB, peers))] * 2
        + copies_of(group)
        + copies_of(floors)
        + [
            pltpu.SemaphoreType.DMA((blocks,)),
            pltpu.SemaphoreType.DMA((slots // LANE,)),
            pltpu.SemaphoreType.DMA,
        ],
        compiler_params=pltpu.CompilerParams(
            vmem_limit_bytes=VMEM_BYTES, collective_id=0, has_side_effects=True
        ),
    )(
        state,
        moments,
        span_owner.reshape(1, columns),
        regime.reshape(1, columns),
        remap_weights,
        remap_rows,
        remap_cols,
    )
    tendencies, moments_out, ocean = pl.pallas_call(
        write_kernel,
        out_shape=(
            jax.ShapeDtypeStruct(state.shape, F32),
            jax.ShapeDtypeStruct(moments.shape, F32),
            jax.ShapeDtypeStruct((share, LANE), F32),
        ),
        in_specs=[whole] * 3,
        out_specs=(whole,) * 3,
        scratch_shapes=[pltpu.SemaphoreType.DMA((1 + blocks + slots // LANE,))],
        compiler_params=params,
    )(*results)
    return (tendencies, moments_out, ocean.reshape(OBLK_DEV, FLUX, LANE))


def solution(mesh):
    return jax.shard_map(
        local,
        mesh=mesh,
        in_specs=(
            P(None, None, ("node", "dev")),
            P(("node", "dev"), None),
            P(("node", "dev")),
            P(None, None, ("node", "dev")),
            P(("node", "dev"), None, None),
            P(("node", "dev")),
            P(("node", "dev")),
        ),
        out_specs=(
            P(None, None, ("node", "dev")),
            P(None, None, ("node", "dev")),
            P(("node", "dev"), None, None),
        ),
        check_vma=False,
    )
```
